512 devices in a mesh: lat: 128 (over y, z, core), ens: 4 (over x).
Axes of the slice: x: 4, y: 4, z: 16, core: 2. Of those that a mesh axis runs over, the one named last changes fastest.
Arguments:
- background: bfloat16 [4, 128, 128, 384], P('ens', 'lat'), may hold values from -6 to 6
- increment: float32 [4, 128, 128, 384], P('ens', 'lat'), may hold values from -4 to 4
- residual: float32 [4, 128, 128, 384], P('ens', 'lat'), may hold values from -120 to 120
- direction: float32 [4, 128, 128, 384], P('ens', 'lat'), may hold values from -120 to 120
- spec_in: float32 [2, 8, 48, 48], replicated, may hold values from -0.625 to 0.625
- spec_out: float32 [2, 8, 48, 48], replicated, may hold values from -0.625 to 0.625
- mlp_in: bfloat16 [384, 3072], P(None, ('lat', 'ens')), may hold values from -0.3125 to 0.3125
- mlp_out: bfloat16 [3072, 384], P(('lat', 'ens')), may hold values from -0.109375 to 0.109375
- readout: float32 [384, 128], replicated, may hold values from -0.3125 to 0.3125
- obs_owner: int32 [16384, 1], P('lat'), may hold values from 0 to 127; in each aligned block of 128 rows (0 to 127, 128 to 255, ...) at most 2 rows name the same one
- obs_cell: int32 [16384], P('lat'), may hold values from 0 to 127
- obs_count: int32 [128], P('lat'), may hold values from 96 to 128, as said below
- obs_weight: float32 [16384, 128], P('lat'), may hold values from 0.5 to 8
Outputs:
- increment_new: float32 [4, 128, 128, 384], P('ens', 'lat')
- residual_new: float32 [4, 128, 128, 384], P('ens', 'lat')
- direction_new: float32 [4, 128, 128, 384], P('ens', 'lat')
- hessian_dir: float32 [4, 128, 128, 384], P('ens', 'lat')
The draws below stay inside these ranges and needn't reach their ends.
Inputs may be any that keep to these rules, and one draw needn't show every extreme that they name: `obs_owner`: in the rows of one instrument owner, at most 2 refer to cells of one latitude owner. `obs_count`: rows of an instrument owner at or past its count carry no observation.
All inputs are finite; a program needn't handle non-finite values.
Results may differ from the reference program's by a relative error of at most 0.017.
Values may be sent and summed in bfloat16 or wider, within the bound.
A program may use at most 64 MiB of HBM per device.

```python
import math
import jax
import jax.numpy as jnp
import numpy as np
from jax import lax

C = 384
FF = 3072
NBLK = 8
BS = 48
NLON = 128
NLAT = 128
CELLS_DEV = 128
MEMBERS = 4
NCH = 128
OBS_DEV = 128
NOBS = 16384
CAP = 2
N_LAT = 128


def layered_field(key, base, rise, spread):
    key_rows, key_chan = jax.random.split(key, 2)
    position = jnp.arange(NLAT, dtype=jnp.float32) / max(NLAT - 1, 1)
    growth = jnp.exp(math.log(rise) * position)[None, :, None, None]
    row_scale = jnp.exp(jax.random.uniform(key_rows, (MEMBERS, NLAT, 1, 1), jnp.float32, -spread, spread))
    chan_scale = jnp.exp(jax.random.uniform(key_chan, (1, 1, 1, C), jnp.float32, -spread, spread))
    return 0.3 * base * growth * row_scale * chan_scale


def draw_residual(key, part):
    key = jax.random.fold_in(key, 11)
    key_base, key_rest = jax.random.split(key)
    base = jnp.clip(jax.random.normal(key_base, (MEMBERS, NLAT, NLON, C), jnp.float32), -4.0, 4.0)
    return layered_field(key_rest, base, 3.0, 1.15)


def draw_direction(key, part):
    key = jax.random.fold_in(key, 12)
    key_base, key_rest = jax.random.split(key)
    base = jnp.clip(jax.random.normal(key_base, (MEMBERS, NLAT, NLON, C), jnp.float32), -4.0, 4.0)
    return layered_field(key_rest, base, 3.0, 1.15)


def draw_obs_count(key, part):
    key = jax.random.fold_in(key, 13)
    key_counts, key_full = jax.random.split(key)
    counts = jax.random.randint(key_counts, (N_LAT,), 3 * OBS_DEV // 4, OBS_DEV + 1, dtype=jnp.int32)
    full_owner = jax.random.randint(key_full, (), 0, N_LAT, dtype=jnp.int32)
    return counts.at[full_owner].set(OBS_DEV)


def touch_ends(array, key, least, largest):
    shape = array.shape
    index_at = [jax.random.randint(jax.random.fold_in(key, axis), (), 0, shape[axis]) for axis in range(len(shape))]
    array = array.at[tuple(index_at)].set(least)
    longest = shape.index(max(shape))
    index_at[longest] = (index_at[longest] + 1) % shape[longest]
    return array.at[tuple(index_at)].set(largest)


def block_levels(stream_key, dims, pieces, least, largest):
    def one(dim, parts):
        steps = jax.random.uniform(jax.random.fold_in(jax.random.fold_in(stream_key, 6), dim), (parts,), jnp.float32, least / len(pieces), largest / len(pieces))
        return jnp.repeat(jnp.exp(steps), dims[dim] // parts).reshape((-1,) + (1,) * (len(dims) - dim - 1))

    level = one(*pieces[0])
    for cut in pieces[1:]:
        level = level * one(*cut)
    return level


def deal_out(own_key, own, number, rows, count, top, limit, lean):
    order = jax.random.permutation(own_key, count)
    packed, ordinary = load_shares(count, rows * top, limit, lean, True), load_shares(count, rows * top, limit, lean, False)
    places = jnp.arange(count)

    def named(tallies, turn):
        used = int((tallies > 0).sum())
        fixed = max(1, used // 4)
        shifted = fixed + (places - fixed + turn * (used - fixed)) % max(1, count - fixed)
        return jnp.zeros((count,), jnp.int32).at[order[jnp.where(places < fixed, places, shifted)]].set(jnp.asarray(tallies, jnp.int32))

    tallies = jnp.where(number % 4 == 0, named(packed, number // 4), named(ordinary, number - number // 4 - 1))
    mixed = jax.random.permutation(jax.random.fold_in(own, 3), count)
    source_of, taker = mixed[0:count // 2 * 2:2], mixed[1:count // 2 * 2:2]
    room = jnp.minimum(tallies[source_of] - 1, limit - tallies[taker]) // 2
    room = jnp.where((source_of == order[0]) | (taker == order[0]) | (tallies[taker] == 0), 0, jnp.maximum(room, 0))
    shifted = jax.random.randint(jax.random.fold_in(own, 4), (count // 2,), 0, 1 << 20) % (room + 1)
    tallies = tallies.at[source_of].add(-shifted).at[taker].add(shifted)
    labels = jnp.searchsorted(jnp.cumsum(tallies), jnp.arange(rows * top), side="right").astype(jnp.int32)
    listing = labels.reshape(top, rows).T
    listing = listing[jax.random.permutation(jax.random.fold_in(own, 1), rows)]
    turn = jax.random.randint(jax.random.fold_in(own, 2), (rows, 1), 0, top)
    return jnp.take_along_axis(listing, (jnp.arange(top)[None, :] + turn) % top, axis=1)


def load_shares(amount, total, limit, lean, full):
    loads = [(1 << 20) // math.isqrt(grade ** lean) + 1 for grade in range(1, amount + 1)]
    largest = limit if full else min(limit, max(-(-total // amount), total * loads[0] // sum(loads)))
    least = 1 if total - largest >= amount - 1 else 0
    given, rest = [largest] + [least] * (amount - 1), total - largest - least * (amount - 1)
    while rest > 0:
        movable = [i for i in range(1, amount) if given[i] < largest] or [i for i in range(1, amount) if given[i] < limit]
        mass, remaining = sum([loads[i] for i in movable]), rest
        for i in movable:
            more = min(limit - given[i], max(1, remaining * loads[i] // mass), rest)
            given[i] = given[i] + more
            rest = rest - more
    return np.array(given)


def bell_draw(stream_key, dims, width, limit, cuts=(), held_as=jnp.bfloat16):
    drawn = jax.random.normal(stream_key, dims, jnp.float32) * width
    if len(cuts) > 0:
        drawn = block_levels(stream_key, dims, cuts, -0.22, 0.18) * drawn
    return jnp.clip(drawn, min=-limit, max=limit).astype(held_as)


def setup_inputs(seed: int = 0) -> dict:
    splits = jax.random.split(jax.random.key(seed), 14)
    background = bell_draw(splits[0], (MEMBERS, NLAT, NLON, C), 1.0, 6.0, ((0, 4), (1, 128)))
    increment = bell_draw(splits[1], (MEMBERS, NLAT, NLON, C), 0.5, 4.0, ((0, 4), (1, 128)), jnp.float32)
    residual = draw_residual(jax.random.fold_in(splits[13], 71), 0)
    direction = draw_direction(jax.random.fold_in(splits[13], 71), 0)
    spec_in = bell_draw(splits[4], (2, NBLK, BS, BS), (2 * BS) ** -0.5, 0.625, (), jnp.float32)
    spec_out = bell_draw(splits[5], (2, NBLK, BS, BS), (2 * BS) ** -0.5, 0.625, (), jnp.float32)
    mlp_in = bell_draw(splits[6], (C, FF), C ** -0.5, 0.3125, ((1, 512),))
    mlp_out = bell_draw(splits[7], (FF, C), FF ** -0.5, 0.109375, ((0, 512),))
    readout = bell_draw(splits[8], (C, NCH), C ** -0.5, 0.3125, (), jnp.float32)
    obs_owner_keys = jax.random.split(jax.random.fold_in(splits[9], 1), NOBS // OBS_DEV)
    obs_owner_turns = jax.random.permutation(jax.random.fold_in(splits[9], 3), NOBS // OBS_DEV)
    obs_owner = jax.vmap(lambda own, number: deal_out(jax.random.fold_in(splits[9], 2), own, number, OBS_DEV, N_LAT, 1, CAP, 1))(obs_owner_keys, obs_owner_turns).reshape((NOBS, 1))
    obs_cell = touch_ends(jax.random.randint(splits[10], (NOBS,), 0, CELLS_DEV), jax.random.fold_in(splits[10], 1), 0, CELLS_DEV - 1).astype(jnp.int32)
    obs_count = draw_obs_count(jax.random.fold_in(splits[13], 71), 0)
    obs_weight = jnp.clip(jnp.exp(math.log(8.0) - 2.7725887 * jax.random.uniform(splits[12], (NOBS, NCH), jnp.float32) ** block_levels(splits[12], (NOBS, NCH), ((0, 128),), -0.2, 0.2)), 0.5, 8.0)
    return {"background": background, "increment": increment, "residual": residual, "direction": direction, "spec_in": spec_in, "spec_out": spec_out, "mlp_in": mlp_in, "mlp_out": mlp_out, "readout": readout, "obs_owner": obs_owner, "obs_cell": obs_cell, "obs_count": obs_count, "obs_weight": obs_weight}


HIGHEST_PRECISION = lax.Precision.HIGHEST
NORM_EPSILON = 1e-05

def layer_norm(values):
    average = lax.optimization_barrier(jnp.mean(values, axis=-1, keepdims=True))
    centred = values - average
    spread = lax.optimization_barrier(jnp.mean(centred * centred, axis=-1, keepdims=True))
    return centred * lax.rsqrt(spread + NORM_EPSILON)

def gelu_value(values):
    return 0.5 * values * (1.0 + lax.erf(values * (1.0 / math.sqrt(2.0))))

def gelu_slope(values):
    cumulative = 0.5 * (1.0 + lax.erf(values * (1.0 / math.sqrt(2.0))))
    density = jnp.exp(-0.5 * values * values) * (1.0 / math.sqrt(2.0 * math.pi))
    return cumulative + values * density

def dft_tables(length):
    positions = jnp.arange(length, dtype=jnp.int32)
    products = positions[:, None] * positions[None, :] % length
    angles = products.astype(jnp.float32) * (2.0 * math.pi / length)
    norm_factor = 1.0 / math.sqrt(length)
    return (jnp.cos(angles) * norm_factor, jnp.sin(angles) * norm_factor)

def lon_forward(values_in, tables):
    cosine, sine_table = tables
    real_part = jnp.einsum('rjc,jl->rlc', values_in, cosine, precision=HIGHEST_PRECISION)
    imag_part = -jnp.einsum('rjc,jl->rlc', values_in, sine_table, precision=HIGHEST_PRECISION)
    return jnp.stack([real_part, imag_part])

def lon_inverse(field_pair, tables):
    cosine, sine_table = tables
    return jnp.einsum('rlc,lj->rjc', field_pair[0], cosine, precision=HIGHEST_PRECISION) - jnp.einsum('rlc,lj->rjc', field_pair[1], sine_table, precision=HIGHEST_PRECISION)

def lat_forward(field_pair, tables):
    cosine, sine_table = tables
    real_part = jnp.einsum('ki,ilc->klc', cosine, field_pair[0], precision=HIGHEST_PRECISION) + jnp.einsum('ki,ilc->klc', sine_table, field_pair[1], precision=HIGHEST_PRECISION)
    imag_part = jnp.einsum('ki,ilc->klc', cosine, field_pair[1], precision=HIGHEST_PRECISION) - jnp.einsum('ki,ilc->klc', sine_table, field_pair[0], precision=HIGHEST_PRECISION)
    return jnp.stack([real_part, imag_part])

def lat_inverse(field_pair, tables):
    cosine, sine_table = tables
    real_part = jnp.einsum('ki,ilc->klc', cosine, field_pair[0], precision=HIGHEST_PRECISION) - jnp.einsum('ki,ilc->klc', sine_table, field_pair[1], precision=HIGHEST_PRECISION)
    imag_part = jnp.einsum('ki,ilc->klc', cosine, field_pair[1], precision=HIGHEST_PRECISION) + jnp.einsum('ki,ilc->klc', sine_table, field_pair[0], precision=HIGHEST_PRECISION)
    return jnp.stack([real_part, imag_part])

def complex_mix(field_pair, weight):
    blocks = weight.shape[1]
    block_size = weight.shape[2]
    shaped = field_pair.reshape(field_pair.shape[:-1] + (blocks, block_size))
    real_part = jnp.einsum('...bd,bde->...be', shaped[0], weight[0], precision=HIGHEST_PRECISION) - jnp.einsum('...bd,bde->...be', shaped[1], weight[1], precision=HIGHEST_PRECISION)
    imag_part = jnp.einsum('...bd,bde->...be', shaped[1], weight[0], precision=HIGHEST_PRECISION) + jnp.einsum('...bd,bde->...be', shaped[0], weight[1], precision=HIGHEST_PRECISION)
    return jnp.stack([real_part, imag_part]).reshape(field_pair.shape)

def complex_mix_adjoint(field_pair, weight):
    blocks = weight.shape[1]
    block_size = weight.shape[2]
    shaped = field_pair.reshape(field_pair.shape[:-1] + (blocks, block_size))
    real_part = jnp.einsum('...be,bde->...bd', shaped[0], weight[0], precision=HIGHEST_PRECISION) + jnp.einsum('...be,bde->...bd', shaped[1], weight[1], precision=HIGHEST_PRECISION)
    imag_part = jnp.einsum('...be,bde->...bd', shaped[1], weight[0], precision=HIGHEST_PRECISION) - jnp.einsum('...be,bde->...bd', shaped[0], weight[1], precision=HIGHEST_PRECISION)
    return jnp.stack([real_part, imag_part]).reshape(field_pair.shape)

def reference(background, increment, residual, direction, spec_in, spec_out, mlp_in, mlp_out, readout, obs_owner, obs_cell, obs_count, obs_weight):
    row_index = jnp.arange(NOBS, dtype=jnp.int32)
    grid_index = (obs_owner[:, 0] * CELLS_DEV + obs_cell).astype(jnp.int32)
    observed = row_index % OBS_DEV < obs_count[row_index // OBS_DEV]
    weights = jnp.where(observed[:, None], obs_weight, 0.0)
    lon_tables = dft_tables(NLON)
    lat_tables = dft_tables(NLAT)
    tokens_all = NLAT * NLON

    def member_product(member_pair):
        state_field = member_pair[0].astype(jnp.float32)
        heading = member_pair[1]
        normed, first_pull = jax.vjp(layer_norm, state_field)
        spectrum = lat_forward(lon_forward(normed, lon_tables), lat_tables)
        before = complex_mix(spectrum, spec_in)
        spec_slope = gelu_slope(before)
        filtered = lon_inverse(lat_inverse(complex_mix(gelu_value(before), spec_out), lat_tables), lon_tables)
        middle = state_field + filtered
        mixed_norm, second_pull = jax.vjp(layer_norm, middle)
        mixed_low = mixed_norm.reshape(tokens_all, C).astype(jnp.bfloat16)
        pre_act = jnp.dot(mixed_low, mlp_in, preferred_element_type=jnp.float32)
        mlp_slope = gelu_slope(pre_act)
        tangent_normed = jax.jvp(layer_norm, (state_field,), (heading,))[1]
        tangent_spec = complex_mix(lat_forward(lon_forward(tangent_normed, lon_tables), lat_tables), spec_in)
        tangent_filtered = lon_inverse(lat_inverse(complex_mix(spec_slope * tangent_spec, spec_out), lat_tables), lon_tables)
        tangent_middle = heading + tangent_filtered
        tangent_mixed = jax.jvp(layer_norm, (middle,), (tangent_middle,))[1].reshape(tokens_all, C).astype(jnp.bfloat16)
        tangent_hidden = (mlp_slope * jnp.dot(tangent_mixed, mlp_in, preferred_element_type=jnp.float32)).astype(jnp.bfloat16)
        tangent_out = tangent_middle.reshape(tokens_all, C) + jnp.dot(tangent_hidden, mlp_out, preferred_element_type=jnp.float32)
        departures = jnp.dot(tangent_out[grid_index], readout, precision=HIGHEST_PRECISION)
        pulled = jnp.dot(weights * departures, readout.T, precision=HIGHEST_PRECISION)
        gradient = jnp.zeros((tokens_all, C), jnp.float32).at[grid_index].add(pulled)
        grad_hidden = jnp.dot(gradient.astype(jnp.bfloat16), mlp_out.T, preferred_element_type=jnp.float32)
        grad_pre = (mlp_slope * grad_hidden).astype(jnp.bfloat16)
        grad_mixed = jnp.dot(grad_pre, mlp_in.T, preferred_element_type=jnp.float32).reshape(NLAT, NLON, C)
        grad_middle = gradient.reshape(NLAT, NLON, C) + second_pull(grad_mixed)[0]
        grad_spec = spec_slope * complex_mix_adjoint(lat_forward(lon_forward(grad_middle, lon_tables), lat_tables), spec_out)
        grad_normed = lon_inverse(lat_inverse(complex_mix_adjoint(grad_spec, spec_in), lat_tables), lon_tables)
        return heading + grad_middle + first_pull(grad_normed)[0]
    hessian_dir = lax.map(member_product, (background, direction))
    norm_now = jnp.sum(residual * residual)
    curvature = jnp.sum(direction * hessian_dir)
    step_size = norm_now / curvature
    increment_new = increment + step_size * direction
    residual_new = residual - step_size * hessian_dir
    norm_next = jnp.sum(residual_new * residual_new)
    direction_new = residual_new + norm_next / norm_now * direction
    return (increment_new, residual_new, direction_new, hessian_dir)
```

```python
import functools
import math

import jax
import jax.numpy as jnp
import numpy as np
from jax import lax
from jax.experimental import pallas as pl
from jax.experimental.pallas import tpu as pltpu
from jax.sharding import PartitionSpec as P

MESH = pl.DeviceIdType.MESH
F32 = jnp.float32
BF16 = jnp.bfloat16
NORM_EPSILON = 1e-05
FEATURES = 384
BLOCK = 48
FIELDS = 7


def split_np(table):
    high = table.astype(np.float32).astype(jnp.bfloat16)
    low = (table - high.astype(np.float64)).astype(np.float32).astype(jnp.bfloat16)
    return high, low


def make_tables(ny, nz):
    chips = ny * nz
    n = 2 * chips
    scale = 1.0 / math.sqrt(n)
    pos = np.arange(n)
    angle = 2.0 * math.pi * ((pos[:, None] * pos[None, :]) % n) / n
    cosine, sine = np.cos(angle) * scale, np.sin(angle) * scale
    alternate = np.where(pos % 2 == 0, 1.0, -1.0) * scale
    lon_f = np.concatenate([cosine[:chips], -sine[:chips]], 0)
    lon_f[chips] = alternate
    y, z, a = np.meshgrid(np.arange(ny), np.arange(nz), np.arange(2), indexing="ij")
    row = (y * nz + z) * 2 + a
    arrive = row.transpose(1, 0, 2).reshape(-1)
    depart = row.transpose(0, 2, 1).reshape(-1)
    lat_f = np.concatenate([cosine[:, arrive], sine[:, arrive]], 1)
    lat_i = np.concatenate([cosine[depart], sine[depart]], 1)
    freq = (y * nz + z).transpose(1, 0, 2).reshape(-1)
    core = a.transpose(1, 0, 2).reshape(-1)
    imag = -sine[:, freq]
    imag[:, freq == 0] = alternate[:, None]
    lon_i = np.concatenate(
        [
            np.concatenate([np.where(core == b, cosine[:, freq], 0.0), np.where(core == b, imag, 0.0)], 1)
            for b in (0, 1)
        ],
        0,
    )
    group = 2 * ny
    perm = np.zeros((n, n))
    for s in range(group):
        for t in range(nz):
            perm[t * group + s, s * nz + t] = 1.0
    pack = np.zeros((12 * nz, 16 * nz))
    for t in range(nz):
        for u in range(6):
            pack[t * 6 + u, t * 16 + u] = 1.0
            pack[6 * nz + t * 6 + u, t * 16 + 8 + u] = 1.0
    narrow = np.concatenate([*split_np(lon_f), perm.astype(jnp.bfloat16)], 0)
    wide = np.concatenate([*split_np(lat_f), *split_np(lat_i), *split_np(lon_i)], 0)
    return narrow, wide, pack.astype(jnp.bfloat16)


def split(values):
    high = values.astype(BF16)
    return high, (values - high.astype(F32)).astype(BF16)


def dot(left, right):
    return jnp.dot(left, right, preferred_element_type=F32)


def dot_t(left, right):
    return lax.dot_general(left, right, (((1,), (1,)), ((), ())), preferred_element_type=F32)


def dot_3(left, right, op=dot):
    return op(left[0], right[0]) + (op(left[1], right[0]) + op(left[0], right[1]))


def normalise(values):
    centred = values - jnp.mean(values, axis=-1, keepdims=True)
    inverse = lax.rsqrt(jnp.mean(centred * centred, axis=-1, keepdims=True) + NORM_EPSILON)
    return centred * inverse, inverse


def norm_linear(normed, inverse, values):
    along = jnp.mean(normed * values, axis=-1, keepdims=True)
    return inverse * (values - jnp.mean(values, axis=-1, keepdims=True) - normed * along)


def gelu_parts(values):
    cumulative = 0.5 * (1.0 + lax.erf(values * (1.0 / math.sqrt(2.0))))
    density = jnp.exp(-0.5 * values * values) * (1.0 / math.sqrt(2.0 * math.pi))
    return values * cumulative, cumulative + values * density


def swap_parts(values):
    return jnp.concatenate(
        [values[:, 128:256], values[:, 0:128], pltpu.roll(values[:, 256:384], 64, 1)], axis=1
    )


def kernel(
    ny,
    nz,
    nx,
    bg_ref,
    dir_ref,
    res_ref,
    spec_in_ref,
    spec_out_ref,
    mlp_in_ref,
    mlp_out_ref,
    readout_ref,
    owner_ref,
    cell_ref,
    count_ref,
    weight_ref,
    narrow_ref,
    wide_ref,
    pack_ref,
    grad_ref,
    scal_ref,
    s1,
    r1,
    s2,
    r2,
    wz,
    wblock,
    win,
    wout,
    slope_ref,
    mixes,
    arz,
    arc,
    arx,
    parts,
    sems,
    wsems,
    rsems,
):
    n = 2 * ny * nz
    chips = ny * nz
    group = 2 * ny
    lat = lax.axis_index("lat")
    ens = lax.axis_index("ens")
    core = lax.rem(lat, 2)
    chip = lax.div(lat, 2)
    yy = lax.div(chip, nz)
    zz = lax.rem(chip, nz)
    me_yc = yy * 2 + core

    def at_yc(k):
        return {"lat": (lax.div(k, 2) * nz + zz) * 2 + lax.rem(k, 2), "ens": ens}

    def at_z(t):
        return {"lat": (yy * nz + t) * 2 + core, "ens": ens}

    def at_x(t):
        return {"lat": lat, "ens": t}

    z_steps = sorted(range(1, nz), key=lambda s: (-min(s, nz - s), s))
    yc_partners = [lax.rem(me_yc + s, group) for s in range(1, group)]
    z_partners = [lax.rem(zz + s, nz) for s in z_steps]
    x_partners = [lax.rem(ens + s, nx) for s in range(1, nx)]
    y_partners = [lax.rem(yy + s, ny) for s in range(1, ny)]

    barrier = pltpu.get_barrier_semaphore()
    for k in yc_partners:
        pl.semaphore_signal(barrier, inc=1, device_id=at_yc(k), device_id_type=MESH)
    for t in z_partners:
        pl.semaphore_signal(barrier, inc=1, device_id=at_z(t), device_id_type=MESH)
    for t in x_partners:
        pl.semaphore_signal(barrier, inc=1, device_id=at_x(t), device_id_type=MESH)

    def push(source, target, send, recv, where):
        pltpu.make_async_remote_copy(
            src_ref=source,
            dst_ref=target,
            send_sem=send,
            recv_sem=recv,
            device_id=where,
            device_id_type=MESH,
        ).start()

    def arrive(ref, sem):
        pltpu.make_async_copy(ref, ref, sem).wait()

    def phase_one(f):
        for k in yc_partners:
            push(s1.at[f, k], r1.at[f, me_yc], sems.at[f, 0], sems.at[f, 1], at_yc(k))
        pltpu.make_async_copy(s1.at[f, me_yc], r1.at[f, me_yc], sems.at[f, 1]).start()

    def phase_two(f):
        arrive(r1.at[f], sems.at[f, 1])
        turned = dot(perm, r1[f].reshape(n, FEATURES))
        s2[f] = turned.reshape(nz, group, FEATURES).astype(BF16)
        for t in z_partners:
            push(s2.at[f, t], r2.at[f, zz], sems.at[f, 2], sems.at[f, 3], at_z(t))
        pltpu.make_async_copy(s2.at[f, zz], r2.at[f, zz], sems.at[f, 3]).start()

    def received(f):
        arrive(r2.at[f], sems.at[f, 3])
        return r2[f].astype(F32).reshape(n, FEATURES)

    lon_f = (narrow_ref[0:n, :], narrow_ref[n : 2 * n, :])
    perm = narrow_ref[2 * n : 3 * n, :]
    lat_f = (wide_ref[0:n, :], wide_ref[n : 2 * n, :])
    lat_i = (wide_ref[2 * n : 3 * n, :], wide_ref[3 * n : 4 * n, :])
    lon_i = (wide_ref[4 * n : 6 * n, :], wide_ref[6 * n : 8 * n, :])

    lane = lax.broadcasted_iota(jnp.int32, (1, FEATURES), 1)
    low_half = lax.rem(lane, 128) < 64
    tail_real = low_half == (core == 0)
    mask_r = jnp.where(jnp.logical_or(lane < 128, jnp.logical_and(lane >= 256, tail_real)), 1.0, 0.0)
    mask_i = 1.0 - mask_r
    plain = jnp.where(chip == 0, 0.0, 1.0)
    first = 1.0 - plain
    low_lane = lax.broadcasted_iota(jnp.int32, (1, 128), 1) < 64

    def lon_forward(f, field):
        spectrum = dot_3(lon_f, split(field))
        real, imag = spectrum[0:chips], spectrum[chips:n]
        imag_mid = pltpu.roll(imag[:, 128:256], 64, 1)
        real_mid = real[:, 128:256]
        for b in (0, 1):
            if b == 0:
                tiles = [real[:, 0:128], imag[:, 0:128], jnp.where(low_lane, real_mid, imag_mid)]
            else:
                tiles = [real[:, 256:384], imag[:, 256:384], jnp.where(low_lane, imag_mid, real_mid)]
            for i, tile in enumerate(tiles):
                low = tile.astype(BF16)
                for y in range(ny):
                    s1[f, 2 * y + b, :, i * 128 : (i + 1) * 128] = low[y * nz : (y + 1) * nz]

    def lon_inverse(f):
        values = received(f)
        tail = values[:, 256:384]
        stacked = jnp.concatenate(
            [
                jnp.concatenate([values[:, 0:128], tail], axis=1),
                jnp.concatenate([values[:, 128:256], pltpu.roll(tail, 64, 1)], axis=1),
            ],
            axis=0,
        ).astype(BF16)
        out = dot(lon_i[0], stacked) + dot(lon_i[1], stacked)
        middle_tile = jnp.where(low_lane, out[0:n, 128:256], out[n : 2 * n, 128:256])
        return jnp.concatenate([out[0:n, 0:128], middle_tile, out[n : 2 * n, 0:128]], axis=1)

    def lat_forward(f):
        x = received(f)
        sw = swap_parts(x)
        left = jnp.concatenate(
            [x * (mask_r + plain * mask_i), sw * (plain * mask_r - mask_i)], axis=0
        ).astype(BF16)
        right = jnp.concatenate(
            [
                x * (plain * mask_r - plain * mask_i) + sw * (first * mask_r),
                sw * (-plain) - x * (first * mask_i),
            ],
            axis=0,
        ).astype(BF16)
        return jnp.concatenate(
            [dot(lat_f[0], left) + dot(lat_f[1], left), dot(lat_f[0], right) + dot(lat_f[1], right)],
            axis=0,
        )

    def lat_inverse(f, both):
        a, b = both[0:n], both[n : 2 * n]
        sa, sb = swap_parts(a), swap_parts(b)
        upper = a * (mask_r + plain * mask_i) + b * (plain * (mask_r - mask_i)) + sb * (first * mask_i)
        lower = sa * (plain * mask_i - mask_r) - sb * plain - b * (first * mask_i)
        out = dot_3(lat_i, split(jnp.concatenate([upper, lower], axis=0)))
        s1[f] = out.reshape(group, nz, FEATURES).astype(BF16)

    def mix(values, which, op=dot):
        return dot_3(split(values), (mixes[2 * which], mixes[2 * which + 1]), op)

    state = bg_ref[...].astype(F32)
    heading = dir_ref[...]
    normed, inverse = normalise(state)
    lon_forward(0, normed)
    pick = lax.broadcasted_iota(jnp.int32, (16, 6), 0) - lax.broadcasted_iota(jnp.int32, (16, 6), 1)
    rows_in = dot_t(jnp.where(pick == 0, 1.0, 0.0).astype(BF16), mlp_in_ref[...])
    rows_out = dot(jnp.where(pick == 8, 1.0, 0.0).astype(BF16), mlp_out_ref[...])
    wblock[...] = (rows_in + rows_out).astype(BF16)

    pl.semaphore_wait(barrier, (group - 1) + (nz - 1) + (nx - 1))
    phase_one(0)
    for t in z_partners:
        push(wblock, wz.at[zz], wsems.at[0], wsems.at[1], at_z(t))
    pltpu.make_async_copy(wblock, wz.at[zz], wsems.at[1]).start()
    lon_forward(1, norm_linear(normed, inverse, heading))
    phase_one(1)
    phase_two(0)
    phase_two(1)

    rows = owner_ref.shape[0]
    owner_col = jnp.broadcast_to(owner_ref[...].astype(F32), (rows, rows))
    owner_row = owner_col.T
    cell_col = jnp.broadcast_to(cell_ref[...].astype(F32), (rows, rows)).T
    sub = lax.broadcasted_iota(jnp.int32, (rows, rows), 0)
    col = lax.broadcasted_iota(jnp.int32, (rows, rows), 1)
    again = jnp.where(jnp.logical_and(owner_col == owner_row, sub < col), 1.0, 0.0)
    rank = jnp.sum(again, axis=0, keepdims=True)
    slot = lax.broadcasted_iota(jnp.int32, (n, rows), 0)
    slot_k, slot_z = lax.div(slot, nz), lax.rem(slot, nz)
    slot_lat = (lax.div(slot_k, 2) * nz + slot_z) * 2 + lax.rem(slot_k, 2)
    mine = owner_row[0:1, :] == slot_lat.astype(F32)
    hit_a = jnp.where(jnp.logical_and(mine, rank == 0.0), 1.0, 0.0).astype(BF16)
    hit_b = jnp.where(jnp.logical_and(mine, rank == 1.0), 1.0, 0.0).astype(BF16)
    row_id = lax.broadcasted_iota(jnp.int32, weight_ref.shape, 0)
    weights = jnp.where(row_id < count_ref[...], weight_ref[...], 0.0).astype(BF16)
    cells = jnp.broadcast_to(cell_col[:, 0:1], (rows, 128)).astype(BF16)
    ids = jnp.where(low_lane, dot(hit_a, cells), dot(hit_b, cells))
    slots = jnp.concatenate([dot(hit_a, weights), dot(hit_b, weights), ids], axis=1)
    s1[2] = slots.reshape(group, nz, FEATURES).astype(BF16)
    phase_one(2)

    half = 4 * BLOCK
    p_row = lax.broadcasted_iota(jnp.int32, (FEATURES, 1), 0)

    def local_feature(p):
        within = lax.rem(p, 128)
        tail = lax.rem(p, 64)
        low_core = jnp.where(p < 256, within, 128 + tail)
        high_core = jnp.where(p < 256, 64 + within, tail)
        return jnp.where(core == 0, low_core, high_core)

    def block_of(u):
        return lax.div(u, BLOCK)

    row_tail_real = (lax.rem(p_row, 128) < 64) == (core == 0)
    row_real = jnp.logical_or(p_row < 128, jnp.logical_and(p_row >= 256, row_tail_real))
    u_row, u_lane = local_feature(p_row), local_feature(lane)
    spread = jnp.where(
        u_row == lax.broadcasted_iota(jnp.int32, (FEATURES, half), 1), 1.0, 0.0
    ).astype(BF16)
    widen = jnp.where(
        lax.broadcasted_iota(jnp.int32, (BLOCK, FEATURES), 0) == u_lane - BLOCK * block_of(u_lane), 1.0, 0.0
    ).astype(BF16)
    same_block = block_of(u_row) == block_of(u_lane)
    same_part = row_real == (mask_r > 0.5)
    cross_sign = jnp.where(row_real, 1.0, -1.0)
    for which, ref in ((0, spec_in_ref), (1, spec_out_ref)):
        real_pair = split(ref[0, pl.ds(core * half, half), :])
        imag_pair = split(ref[1, pl.ds(core * half, half), :])
        for level in (0, 1):
            real_part = dot(dot(spread, real_pair[level]).astype(BF16), widen)
            imag_part = dot(dot(spread, imag_pair[level]).astype(BF16), widen)
            dense = jnp.where(same_part, real_part, imag_part * cross_sign)
            mixes[2 * which + level] = jnp.where(same_block, dense, 0.0).astype(BF16)

    six = 6 * nz
    arrive(wz, wsems.at[1])
    packed = dot(pack_ref[...], wz[...].reshape(16 * nz, FEATURES)).astype(BF16)
    win[core, ens, yy] = packed[0:six]
    wout[core, ens, yy] = packed[six : 2 * six]
    for y in y_partners:
        push(win.at[core, ens, yy], win.at[core, ens, yy], wsems.at[2], wsems.at[3], at_yc(y * 2 + core))
    for t in x_partners:
        push(wout.at[core, ens, yy], wout.at[core, ens, yy], wsems.at[4], wsems.at[5], at_x(t))

    before = mix(lat_forward(0), 0)
    value, spec_slope = gelu_parts(before)
    lat_inverse(3, mix(value, 1))
    phase_one(3)

    sibling = at_yc(yy * 2 + (1 - core))
    arrive(win.at[0, 0, pl.ds(0, ny - 1)], wsems.at[3])
    for t in x_partners:
        push(win.at[core, ens], win.at[core, ens], wsems.at[6], wsems.at[7], at_x(t))
    push(win.at[core, ens], win.at[core, ens], wsems.at[10], wsems.at[11], sibling)
    arrive(wout.at[0, 0, pl.ds(0, nx - 1)], wsems.at[5])
    for y in y_partners:
        push(wout.at[core, :, yy], wout.at[core, :, yy], wsems.at[8], wsems.at[9], at_yc(y * 2 + core))
    push(wout.at[core, :, yy], wout.at[core, :, yy], wsems.at[12], wsems.at[13], sibling)

    lat_inverse(4, mix(spec_slope * mix(lat_forward(1), 0), 1))
    phase_one(4)
    phase_two(3)
    phase_two(2)
    phase_two(4)

    middle = state + lon_inverse(3)
    mixed, mixed_inverse = normalise(middle)
    mixed_low = mixed.astype(BF16)

    arrive(win.at[0, pl.ds(0, nx - 1)], wsems.at[7])
    for t in x_partners:
        push(win.at[core, t], win.at[core, t], wsems.at[10], wsems.at[11], sibling)
    arrive(wout.at[0, pl.ds(0, ny - 1)], wsems.at[9])
    for y in y_partners:
        push(wout.at[core, :, y], wout.at[core, :, y], wsems.at[12], wsems.at[13], sibling)

    got = received(2)
    cell_id = lax.broadcasted_iota(jnp.int32, (n, n), 1).astype(F32)
    at_a = jnp.where(got[:, 256:257] == cell_id, 1.0, 0.0)
    at_b = jnp.where(got[:, 320:321] == cell_id, 1.0, 0.0)
    cell_weights = dot(at_a.T.astype(BF16), got[:, 0:128].astype(BF16)) + dot(
        at_b.T.astype(BF16), got[:, 128:256].astype(BF16)
    )

    units = ny * six
    arrive(win.at[0], wsems.at[11])

    def slope_step(i, carry):
        block = win[lax.div(i, nx), lax.rem(i, nx)].reshape(units, FEATURES)
        slope_ref[i] = gelu_parts(dot_t(mixed_low, block))[1]
        return carry

    lax.fori_loop(0, 2 * nx, slope_step, 0)

    tangent_middle = heading + lon_inverse(4)
    tangent_low = norm_linear(mixed, mixed_inverse, tangent_middle).astype(BF16)
    arrive(wout.at[0], wsems.at[13])

    def tangent_step(i, total):
        co, t = lax.div(i, nx), lax.rem(i, nx)
        block_in = win[co, t].reshape(units, FEATURES)
        block_out = wout[co, t].reshape(units, FEATURES)
        hidden = (slope_ref[i] * dot_t(tangent_low, block_in)).astype(BF16)
        return total + dot(hidden, block_out)

    tangent_out = lax.fori_loop(0, 2 * nx, tangent_step, tangent_middle)

    readout = split(readout_ref[...])
    departures = dot_3(split(tangent_out), readout)
    gradient = dot_3(split(cell_weights * departures), readout, dot_t)
    gradient_low = gradient.astype(BF16)

    def grad_step(i, total):
        co, t = lax.div(i, nx), lax.rem(i, nx)
        block_in = win[co, t].reshape(units, FEATURES)
        block_out = wout[co, t].reshape(units, FEATURES)
        grad_pre = (slope_ref[i] * dot_t(gradient_low, block_out)).astype(BF16)
        return total + dot(grad_pre, block_in)

    grad_mixed = lax.fori_loop(0, 2 * nx, grad_step, jnp.zeros((n, FEATURES), F32))
    grad_middle = gradient + norm_linear(mixed, mixed_inverse, grad_mixed)

    lon_forward(5, grad_middle)
    phase_one(5)
    phase_two(5)
    lat_inverse(6, mix(spec_slope * mix(lat_forward(5), 1, dot_t), 0, dot_t))
    phase_one(6)
    phase_two(6)
    update = grad_middle + norm_linear(normed, inverse, lon_inverse(6))
    grad_ref[...] = update

    residual = res_ref[...]
    hessian = heading + update
    sums = [
        jnp.sum(jnp.sum(v, axis=0, keepdims=True), axis=1, keepdims=True)
        for v in (residual * residual, heading * hessian, residual * hessian, hessian * hessian)
    ]
    which = lax.broadcasted_iota(jnp.int32, (8, 128), 0)
    total = jnp.zeros((8, 128), F32)
    for i, value in enumerate(sums):
        total = total + jnp.where(which == i, value, 0.0)

    def reduce_over(i, total, buffer, mine_at, partners, where):
        parts[i] = total
        for t in partners:
            push(parts.at[i], buffer.at[mine_at], rsems.at[i, 0], rsems.at[i, 1], where(t))
        pltpu.make_async_copy(parts.at[i], buffer.at[mine_at], rsems.at[i, 1]).start()
        arrive(buffer, rsems.at[i, 1])
        return jnp.sum(buffer[...], axis=0)

    total = reduce_over(0, total, arz, zz, z_partners, at_z)
    total = reduce_over(1, total, arc, me_yc, yc_partners, at_yc)
    total = reduce_over(2, total, arx, ens, x_partners, at_x)
    norm_now, curvature, cross, square = total[0:1], total[1:2], total[2:3], total[3:4]
    step = norm_now / curvature
    norm_next = norm_now + step * (step * square - 2.0 * cross)
    ratio = norm_next / norm_now
    scal_ref[...] = jnp.where(which == 0, step, ratio)

    for f in range(FIELDS):
        arrive(s1.at[f, pl.ds(0, group - 1)], sems.at[f, 0])
        arrive(s2.at[f, pl.ds(0, nz - 1)], sems.at[f, 2])
    arrive(wz.at[pl.ds(0, nz - 1)], wsems.at[0])
    arrive(win.at[0, 0, pl.ds(0, ny - 1)], wsems.at[2])
    arrive(wout.at[0, 0, pl.ds(0, nx - 1)], wsems.at[4])
    arrive(win.at[0, pl.ds(0, nx - 1)], wsems.at[6])
    arrive(wout.at[0, pl.ds(0, ny - 1)], wsems.at[8])
    arrive(win.at[0], wsems.at[10])
    arrive(wout.at[0], wsems.at[12])
    arrive(arz.at[pl.ds(0, nz - 1)], rsems.at[0, 0])
    arrive(arc.at[pl.ds(0, group - 1)], rsems.at[1, 0])
    arrive(arx.at[pl.ds(0, nx - 1)], rsems.at[2, 0])


def per_device(ny, nz, nx, background, increment, residual, direction, spec_in, spec_out, mlp_in,
               mlp_out, readout, obs_owner, obs_cell, obs_count, obs_weight):
    n = background.shape[2]
    group = 2 * ny
    six = 6 * nz
    narrow, wide, pack = make_tables(ny, nz)
    vmem = pl.BlockSpec(memory_space=pltpu.VMEM)
    update, scal = pl.pallas_call(
        functools.partial(kernel, ny, nz, nx),
        out_shape=(
            jax.ShapeDtypeStruct((n, FEATURES), F32),
            jax.ShapeDtypeStruct((8, 128), F32),
        ),
        in_specs=[vmem] * 15,
        out_specs=(vmem, vmem),
        scratch_shapes=[
            pltpu.VMEM((FIELDS, group, nz, FEATURES), BF16),
            pltpu.VMEM((FIELDS, group, nz, FEATURES), BF16),
            pltpu.VMEM((FIELDS, nz, group, FEATURES), BF16),
            pltpu.VMEM((FIELDS, nz, group, FEATURES), BF16),
            pltpu.VMEM((nz, 16, FEATURES), BF16),
            pltpu.VMEM((16, FEATURES), BF16),
            pltpu.VMEM((2, nx, ny, six, FEATURES), BF16),
            pltpu.VMEM((2, nx, ny, six, FEATURES), BF16),
            pltpu.VMEM((2 * nx, n, ny * six), F32),
            pltpu.VMEM((4, FEATURES, FEATURES), BF16),
            pltpu.VMEM((nz, 8, 128), F32),
            pltpu.VMEM((group, 8, 128), F32),
            pltpu.VMEM((nx, 8, 128), F32),
            pltpu.VMEM((3, 8, 128), F32),
            pltpu.SemaphoreType.DMA((FIELDS, 4)),
            pltpu.SemaphoreType.DMA((14,)),
            pltpu.SemaphoreType.DMA((3, 2)),
        ],
        compiler_params=pltpu.CompilerParams(
            collective_id=0, has_side_effects=True, vmem_limit_bytes=48 * 1024 * 1024
        ),
    )(
        background.reshape(n, FEATURES),
        direction.reshape(n, FEATURES),
        residual.reshape(n, FEATURES),
        spec_in.reshape(2, FEATURES, BLOCK),
        spec_out.reshape(2, FEATURES, BLOCK),
        mlp_in,
        mlp_out,
        readout,
        obs_owner,
        obs_cell.reshape(1, -1),
        obs_count.reshape(1, 1),
        obs_weight,
        jnp.asarray(narrow),
        jnp.asarray(wide),
        jnp.asarray(pack),
    )
    step, ratio = scal[0, 0], scal[1, 0]
    hessian_dir = direction + update.reshape(direction.shape)
    residual_new = residual - step * hessian_dir
    return (
        increment + step * direction,
        residual_new,
        residual_new + ratio * direction,
        hessian_dir,
    )


def solution(mesh):
    n_lat, nx = mesh.shape["lat"], mesh.shape["ens"]
    nz = 16 if n_lat == 128 else 2
    ny = n_lat // (2 * nz)
    field = P("ens", "lat", None, None)
    return jax.shard_map(
        functools.partial(per_device, ny, nz, nx),
        mesh=mesh,
        in_specs=(
            field,
            field,
            field,
            field,
            P(),
            P(),
            P(None, ("lat", "ens")),
            P(("lat", "ens"), None),
            P(),
            P("lat", None),
            P("lat"),
            P("lat"),
            P("lat", None),
        ),
        out_specs=(field, field, field, field),
        check_vma=False,
    )
```

```python
import functools
import math

import jax
import jax.numpy as jnp
import numpy as np
from jax import lax
from jax.experimental import pallas as pl
from jax.experimental.pallas import tpu as pltpu
from jax.sharding import PartitionSpec as P

MESH = pl.DeviceIdType.MESH
F32 = jnp.float32
BF16 = jnp.bfloat16
NORM_EPSILON = 1e-05
FEATURES = 384
BLOCK = 48
FIELDS = 7


def split_np(table):
    high = table.astype(np.float32).astype(jnp.bfloat16)
    low = (table - high.astype(np.float64)).astype(np.float32).astype(jnp.bfloat16)
    return high, low


def make_tables(ny, nz):
    chips = ny * nz
    n = 2 * chips
    scale = 1.0 / math.sqrt(n)
    pos = np.arange(n)
    angle = 2.0 * math.pi * ((pos[:, None] * pos[None, :]) % n) / n
    cosine, sine = np.cos(angle) * scale, np.sin(angle) * scale
    alternate = np.where(pos % 2 == 0, 1.0, -1.0) * scale
    lon_f = np.concatenate([cosine[:chips], -sine[:chips]], 0)
    lon_f[chips] = alternate
    y, z, a = np.meshgrid(np.arange(ny), np.arange(nz), np.arange(2), indexing="ij")
    row = (y * nz + z) * 2 + a
    arrive = row.transpose(1, 0, 2).reshape(-1)
    depart = row.transpose(0, 2, 1).reshape(-1)
    lat_f = np.concatenate([cosine[:, arrive], sine[:, arrive]], 1)
    lat_i = np.concatenate([cosine[depart], sine[depart]], 1)
    freq = (y * nz + z).transpose(1, 0, 2).reshape(-1)
    core = a.transpose(1, 0, 2).reshape(-1)
    imag = -sine[:, freq]
    imag[:, freq == 0] = alternate[:, None]
    lon_i = np.concatenate(
        [
            np.concatenate([np.where(core == b, cosine[:, freq], 0.0), np.where(core == b, imag, 0.0)], 1)
            for b in (0, 1)
        ],
        0,
    )
    group = 2 * ny
    perm = np.zeros((n, n))
    for s in range(group):
        for t in range(nz):
            perm[t * group + s, s * nz + t] = 1.0
    pack = np.zeros((12 * nz, 16 * nz))
    for t in range(nz):
        for u in range(6):
            pack[t * 6 + u, t * 16 + u] = 1.0
            pack[6 * nz + t * 6 + u, t * 16 + 8 + u] = 1.0
    narrow = np.concatenate([*split_np(lon_f), perm.astype(jnp.bfloat16)], 0)
    wide = np.concatenate([*split_np(lat_f), *split_np(lat_i), *split_np(lon_i)], 0)
    return narrow, wide, pack.astype(jnp.bfloat16)


def split(values):
    high = values.astype(BF16)
    return high, (values - high.astype(F32)).astype(BF16)


def dot(left, right):
    return jnp.dot(left, right, preferred_element_type=F32)


def dot_t(left, right):
    return lax.dot_general(left, right, (((1,), (1,)), ((), ())), preferred_element_type=F32)


def dot_3(left, right, op=dot):
    return op(left[0], right[0]) + (op(left[1], right[0]) + op(left[0], right[1]))


def normalise(values):
    centred = values - jnp.mean(values, axis=-1, keepdims=True)
    inverse = lax.rsqrt(jnp.mean(centred * centred, axis=-1, keepdims=True) + NORM_EPSILON)
    return centred * inverse, inverse


def norm_linear(normed, inverse, values):
    along = jnp.mean(normed * values, axis=-1, keepdims=True)
    return inverse * (values - jnp.mean(values, axis=-1, keepdims=True) - normed * along)


def gelu_parts(values):
    cumulative = 0.5 * (1.0 + lax.erf(values * (1.0 / math.sqrt(2.0))))
    density = jnp.exp(-0.5 * values * values) * (1.0 / math.sqrt(2.0 * math.pi))
    return values * cumulative, cumulative + values * density


def swap_parts(values):
    return jnp.concatenate(
        [values[:, 128:256], values[:, 0:128], pltpu.roll(values[:, 256:384], 64, 1)], axis=1
    )


def kernel(
    ny,
    nz,
    nx,
    *refs,
):
    inputs, (grad_ref, scal_ref), held, rest = refs[:15], refs[15:17], refs[17:32], refs[32:]
    (
        bg_ref,
        narrow_ref,
        dir_ref,
        mlp_in_ref,
        mlp_out_ref,
        wide_ref,
        spec_in_ref,
        spec_out_ref,
        pack_ref,
        owner_ref,
        cell_ref,
        count_ref,
        weight_ref,
        readout_ref,
        res_ref,
    ) = held
    (
        s1,
        r1,
        s2,
        r2,
        wz,
        win,
        wout,
        slope_ref,
        mixes,
        around,
        along,
        parts,
        sems,
        zsems,
        wsems,
        rsems,
        insems,
    ) = rest
    n = 2 * ny * nz
    chips = ny * nz
    group = 2 * ny
    lat = lax.axis_index("lat")
    ens = lax.axis_index("ens")
    core = lax.rem(lat, 2)
    chip = lax.div(lat, 2)
    yy = lax.div(chip, nz)
    zz = lax.rem(chip, nz)
    me_yc = yy * 2 + core

    def at_yc(k):
        return {"lat": (lax.div(k, 2) * nz + zz) * 2 + lax.rem(k, 2), "ens": ens}

    def at_z(t):
        return {"lat": (yy * nz + t) * 2 + core, "ens": ens}

    def at_x(t):
        return {"lat": lat, "ens": t}

    z_steps = sorted(range(1, nz), key=lambda s: (-min(s, nz - s), s))
    yc_partners = [lax.rem(me_yc + s, group) for s in range(1, group)]
    z_partners = [lax.rem(zz + s, nz) for s in z_steps]
    plane = [
        (lax.rem(me_yc + k, group), lax.rem(ens + t, nx))
        for k, t in sorted(
            ((k, t) for k in range(group) for t in range(nx) if k or t),
            key=lambda p: -min(p[0] // 2, ny - p[0] // 2) - min(p[1], nx - p[1]),
        )
    ]

    def at_plane(p):
        return {"lat": (lax.div(p[0], 2) * nz + zz) * 2 + lax.rem(p[0], 2), "ens": p[1]}

    for i in range(15):
        pltpu.make_async_copy(inputs[i], held[i], insems.at[i]).start()
    barrier = pltpu.get_barrier_semaphore()
    for t in z_partners:
        pl.semaphore_signal(barrier, inc=1, device_id=at_z(t), device_id_type=MESH)
    for p in plane:
        pl.semaphore_signal(barrier, inc=1, device_id=at_plane(p), device_id_type=MESH)

    ready = set()

    def load(*wanted):
        for ref in wanted:
            i = next(k for k in range(15) if held[k] is ref)
            if i not in ready:
                ready.add(i)
                pltpu.make_async_copy(inputs[i], ref, insems.at[i]).wait()

    leaving, coming = [], {}

    def push(source, target, send, recv, where):
        pltpu.make_async_remote_copy(
            src_ref=source,
            dst_ref=target,
            send_sem=send,
            recv_sem=recv,
            device_id=where,
            device_id_type=MESH,
        ).start()

    def wait_bytes(ref, sem):
        pltpu.make_async_copy(ref, ref, sem).wait()

    def arrive(key):
        wait_bytes(*coming.pop(key))

    def finish():
        load(*held)
        for key in list(coming):
            arrive(key)
        for ref, sem in leaving:
            wait_bytes(ref, sem)

    def phase_one(f):
        for k in yc_partners:
            push(s1.at[f, k], r1.at[f, me_yc], sems.at[f, 0], sems.at[f, 1], at_yc(k))
        pltpu.make_async_copy(s1.at[f, me_yc], r1.at[f, me_yc], sems.at[f, 1]).start()
        leaving.append((s1.at[f, pl.ds(0, group - 1)], sems.at[f, 0]))
        coming["one", f] = (r1.at[f], sems.at[f, 1])

    def phase_two(f):
        arrive(("one", f))
        turned = dot(narrow_ref[2 * n : 3 * n, :], r1[f].reshape(n, FEATURES))
        s2[f] = turned.reshape(nz, group, FEATURES).astype(BF16)
        for t in z_partners:
            push(s2.at[f, t], r2.at[f, zz], sems.at[f, 2], sems.at[f, 3], at_z(t))
        pltpu.make_async_copy(s2.at[f, zz], r2.at[f, zz], sems.at[f, 3]).start()
        leaving.append((s2.at[f, pl.ds(0, nz - 1)], sems.at[f, 2]))
        coming["two", f] = (r2.at[f], sems.at[f, 3])

    def received(f):
        arrive(("two", f))
        return r2[f].astype(F32).reshape(n, FEATURES)

    def lon_f():
        load(narrow_ref)
        return narrow_ref[0:n, :], narrow_ref[n : 2 * n, :]

    def lat_f():
        load(wide_ref)
        return wide_ref[0:n, :], wide_ref[n : 2 * n, :]

    def lat_i():
        return wide_ref[2 * n : 3 * n, :], wide_ref[3 * n : 4 * n, :]

    def lon_i():
        return wide_ref[4 * n : 6 * n, :], wide_ref[6 * n : 8 * n, :]

    lane = lax.broadcasted_iota(jnp.int32, (1, FEATURES), 1)
    low_half = lax.rem(lane, 128) < 64
    tail_real = low_half == (core == 0)
    mask_r = jnp.where(jnp.logical_or(lane < 128, jnp.logical_and(lane >= 256, tail_real)), 1.0, 0.0)
    mask_i = 1.0 - mask_r
    plain = jnp.where(chip == 0, 0.0, 1.0)
    first = 1.0 - plain
    low_lane = lax.broadcasted_iota(jnp.int32, (1, 128), 1) < 64

    def lon_forward(f, field):
        spectrum = dot_3(lon_f(), split(field))
        real, imag = spectrum[0:chips], spectrum[chips:n]
        imag_mid = pltpu.roll(imag[:, 128:256], 64, 1)
        real_mid = real[:, 128:256]
        for b in (0, 1):
            if b == 0:
                tiles = [real[:, 0:128], imag[:, 0:128], jnp.where(low_lane, real_mid, imag_mid)]
            else:
                tiles = [real[:, 256:384], imag[:, 256:384], jnp.where(low_lane, imag_mid, real_mid)]
            for i, tile in enumerate(tiles):
                low = tile.astype(BF16)
                for y in range(ny):
                    s1[f, 2 * y + b, :, i * 128 : (i + 1) * 128] = low[y * nz : (y + 1) * nz]

    def lon_inverse(f):
        values = received(f)
        tail = values[:, 256:384]
        stacked = jnp.concatenate(
            [
                jnp.concatenate([values[:, 0:128], tail], axis=1),
                jnp.concatenate([values[:, 128:256], pltpu.roll(tail, 64, 1)], axis=1),
            ],
            axis=0,
        ).astype(BF16)
        high, low = lon_i()
        out = dot(high, stacked) + dot(low, stacked)
        middle_tile = jnp.where(low_lane, out[0:n, 128:256], out[n : 2 * n, 128:256])
        return jnp.concatenate([out[0:n, 0:128], middle_tile, out[n : 2 * n, 0:128]], axis=1)

    def lat_forward(f):
        high, low = lat_f()
        x = received(f)
        sw = swap_parts(x)
        left = jnp.concatenate(
            [x * (mask_r + plain * mask_i), sw * (plain * mask_r - mask_i)], axis=0
        ).astype(BF16)
        right = jnp.concatenate(
            [
                x * (plain * mask_r - plain * mask_i) + sw * (first * mask_r),
                sw * (-plain) - x * (first * mask_i),
            ],
            axis=0,
        ).astype(BF16)
        return jnp.concatenate(
            [dot(high, left) + dot(low, left), dot(high, right) + dot(low, right)],
            axis=0,
        )

    def lat_inverse(f, both):
        a, b = both[0:n], both[n : 2 * n]
        sa, sb = swap_parts(a), swap_parts(b)
        upper = a * (mask_r + plain * mask_i) + b * (plain * (mask_r - mask_i)) + sb * (first * mask_i)
        lower = sa * (plain * mask_i - mask_r) - sb * plain - b * (first * mask_i)
        out = dot_3(lat_i(), split(jnp.concatenate([upper, lower], axis=0)))
        s1[f] = out.reshape(group, nz, FEATURES).astype(BF16)

    def mix(values, which, op=dot):
        return dot_3(split(values), (mixes[2 * which], mixes[2 * which + 1]), op)

    load(bg_ref)
    state = bg_ref[...].astype(F32)
    normed, inverse = normalise(state)
    lon_forward(0, normed)
    pick = lax.broadcasted_iota(jnp.int32, (16, 6), 0) - lax.broadcasted_iota(jnp.int32, (16, 6), 1)
    load(mlp_in_ref, mlp_out_ref)
    rows_in = dot(jnp.where(pick == 0, 1.0, 0.0).astype(BF16), mlp_in_ref[...])
    rows_out = dot(jnp.where(pick == 8, 1.0, 0.0).astype(BF16), mlp_out_ref[...])
    wz[lax.rem(zz, min(4, nz)), lax.div(zz, min(4, nz))] = (rows_in + rows_out).astype(BF16)
    load(dir_ref)
    heading = dir_ref[...]
    lon_forward(1, norm_linear(normed, inverse, heading))
    load(owner_ref, cell_ref, count_ref, weight_ref)
    rows = owner_ref.shape[1]
    owner_row = jnp.broadcast_to(owner_ref[...].astype(F32), (rows, rows))
    owner_col = owner_row.T
    cell_col = jnp.broadcast_to(cell_ref[...].astype(F32), (rows, rows)).T
    sub = lax.broadcasted_iota(jnp.int32, (rows, rows), 0)
    col = lax.broadcasted_iota(jnp.int32, (rows, rows), 1)
    again = jnp.where(jnp.logical_and(owner_col == owner_row, sub < col), 1.0, 0.0)
    rank = jnp.sum(again, axis=0, keepdims=True)
    slot = lax.broadcasted_iota(jnp.int32, (n, rows), 0)
    slot_k, slot_z = lax.div(slot, nz), lax.rem(slot, nz)
    slot_lat = (lax.div(slot_k, 2) * nz + slot_z) * 2 + lax.rem(slot_k, 2)
    mine = owner_row[0:1, :] == slot_lat.astype(F32)
    hit_a = jnp.where(jnp.logical_and(mine, rank == 0.0), 1.0, 0.0).astype(BF16)
    hit_b = jnp.where(jnp.logical_and(mine, rank == 1.0), 1.0, 0.0).astype(BF16)
    row_id = lax.broadcasted_iota(jnp.int32, weight_ref.shape, 0)
    weights = jnp.where(row_id < count_ref[...], weight_ref[...], 0.0).astype(BF16)
    cells = jnp.broadcast_to(cell_col[:, 0:1], (rows, 128)).astype(BF16)
    ids = jnp.where(low_lane, dot(hit_a, cells), dot(hit_b, cells))
    slots = jnp.concatenate([dot(hit_a, weights), dot(hit_b, weights), ids], axis=1)
    s1[2] = slots.reshape(group, nz, FEATURES).astype(BF16)
    pl.semaphore_wait(barrier, (nz - 1) + (group * nx - 1))
    phase_one(0)
    classes = min(4, nz)
    quads = nz // classes
    own_class, own_quad = lax.rem(zz, classes), lax.div(zz, classes)
    far = sorted(range(1, quads), key=lambda q: -min(q, quads - q))
    for q in far:
        target = lax.rem(zz + classes * q, nz)
        push(wz.at[own_class, own_quad], wz.at[own_class, own_quad], zsems.at[0], zsems.at[1], at_z(target))
    if far:
        leaving.append((wz.at[0, pl.ds(0, quads - 1)], zsems.at[0]))
        coming["quads"] = (wz.at[0, pl.ds(0, quads - 1)], zsems.at[1])
    phase_one(1)
    phase_one(2)
    phase_two(0)
    phase_two(1)
    if far:
        arrive("quads")
    near = [1, nz - 1, 2][: classes - 1]
    for step in near:
        push(wz.at[own_class], wz.at[own_class], zsems.at[2], zsems.at[3], at_z(lax.rem(zz + step, nz)))
    if near:
        leaving.append((wz.at[pl.ds(0, classes - 1)], zsems.at[2]))
        coming["classes"] = (wz.at[pl.ds(0, classes - 1)], zsems.at[3])
    phase_two(2)
    half = 4 * BLOCK
    p_row = lax.broadcasted_iota(jnp.int32, (FEATURES, 1), 0)

    def local_feature(p):
        within = lax.rem(p, 128)
        tail = lax.rem(p, 64)
        low_core = jnp.where(p < 256, within, 128 + tail)
        high_core = jnp.where(p < 256, 64 + within, tail)
        return jnp.where(core == 0, low_core, high_core)

    def block_of(u):
        return lax.div(u, BLOCK)

    row_tail_real = (lax.rem(p_row, 128) < 64) == (core == 0)
    row_real = jnp.logical_or(p_row < 128, jnp.logical_and(p_row >= 256, row_tail_real))
    u_row, u_lane = local_feature(p_row), local_feature(lane)
    spread = jnp.where(
        u_row == lax.broadcasted_iota(jnp.int32, (FEATURES, half), 1), 1.0, 0.0
    ).astype(BF16)
    widen = jnp.where(
        lax.broadcasted_iota(jnp.int32, (BLOCK, FEATURES), 0) == u_lane - BLOCK * block_of(u_lane), 1.0, 0.0
    ).astype(BF16)
    same_block = block_of(u_row) == block_of(u_lane)
    same_part = row_real == (mask_r > 0.5)
    cross_sign = jnp.where(row_real, 1.0, -1.0)
    load(spec_in_ref, spec_out_ref)
    for which, ref in ((0, spec_in_ref), (1, spec_out_ref)):
        real_pair = split(ref[0, pl.ds(core * half, half), :])
        imag_pair = split(ref[1, pl.ds(core * half, half), :])
        for level in (0, 1):
            real_part = dot(dot(spread, real_pair[level]).astype(BF16), widen)
            imag_part = dot(dot(spread, imag_pair[level]).astype(BF16), widen)
            dense = jnp.where(same_part, real_part, imag_part * cross_sign)
            mixes[2 * which + level] = jnp.where(same_block, dense, 0.0).astype(BF16)

    six = 6 * nz
    sibling = at_yc(yy * 2 + (1 - core))

    class Gather:
        def __init__(self, ref, which, first, second, first_at, second_at, first_n, second_n):
            self.ref, self.sem, self.f, self.g = ref, lambda i: wsems.at[which, i], first, second
            self.first_at, self.second_at = first_at, second_at
            self.nf, self.ng = first_n, second_n
            self.left = lax.rem(second + second_n - 1, second_n)
            self.right = lax.rem(second + 1, second_n)

        def block(self, g, f):
            return self.ref.at[core, g, f]

        def offset(self, i):
            return lax.rem(self.f + i, self.nf)

        def beside(self, f):
            mine = self.block(self.g, f)
            if self.ng > 1:
                push(mine, mine, self.sem(2), self.sem(3), self.second_at(self.right))
            if self.ng > 2:
                push(mine, mine, self.sem(4), self.sem(5), self.second_at(self.left))

        def begin(self):
            mine = self.block(self.g, self.f)
            for i in range(1, self.nf):
                push(mine, mine, self.sem(0), self.sem(1), self.first_at(self.offset(i)))
            self.beside(self.f)
            if self.nf > 1:
                leaving.append((self.ref.at[0, 0, pl.ds(0, self.nf - 1)], self.sem(0)))
                coming["first", self] = (self.ref.at[0, 0, pl.ds(0, self.nf - 1)], self.sem(1))
            if self.ng > 1:
                leaving.append((self.ref.at[0, 0], self.sem(2)))
                coming["left", self] = (self.ref.at[0, 0], self.sem(3))
            if self.ng > 2:
                leaving.append((self.ref.at[0, 0], self.sem(4)))
                coming["right", self] = (self.ref.at[0, 0], self.sem(5))

        def cross(self, g, i):
            slab = self.ref.at[core, g]
            push(slab, slab, self.sem(8 + 2 * i), self.sem(9 + 2 * i), sibling)
            leaving.append((slab, self.sem(8 + 2 * i)))
            coming["core", self, i] = (slab, self.sem(9 + 2 * i))

        def spread(self):
            if self.nf > 1:
                arrive(("first", self))
            for i in range(1, self.nf):
                self.beside(self.offset(i))

        def cross_own(self):
            self.cross(self.g, 0)

        def pass_on(self):
            for key in ("left", "right"):
                if (key, self) in coming:
                    arrive((key, self))
            if self.ng > 2:
                for i in range(self.nf):
                    ref = self.block(self.left if i % 2 == 0 else self.right, self.offset(i))
                    push(ref, ref, self.sem(6), self.sem(7), self.second_at(self.right if i % 2 == 0 else self.left))
                leaving.append((self.ref.at[0, 0], self.sem(6)))
                coming["opposite", self] = (self.ref.at[0, 0], self.sem(7))
            if self.ng > 1:
                self.cross(self.left, 1)
            if self.ng > 2:
                self.cross(self.right, 2)

        def last(self):
            if self.ng > 2:
                arrive(("opposite", self))
                self.cross(lax.rem(self.g + 2, self.ng), 3)

        def slabs(self):
            return [self.g, self.left, self.right, lax.rem(self.g + 2, self.ng)][: self.ng]

    def at_y(t):
        return at_yc(t * 2 + core)

    gather_in = Gather(win, 0, yy, ens, at_y, at_x, ny, nx)
    gather_out = Gather(wout, 1, ens, yy, at_x, at_y, nx, ny)
    if near:
        arrive("classes")
    load(pack_ref)
    packed = dot(pack_ref[...], wz[...].reshape(16 * nz, FEATURES)).astype(BF16)
    win[core, ens, yy] = packed[0:six]
    wout[core, yy, ens] = packed[six : 2 * six]
    gather_in.begin()
    gather_out.begin()
    before = mix(lat_forward(0), 0)
    value, spec_slope = gelu_parts(before)
    lat_inverse(3, mix(value, 1))
    phase_one(3)

    lat_inverse(4, mix(spec_slope * mix(lat_forward(1), 0), 1))
    phase_one(4)
    gather_in.spread()
    gather_out.spread()
    phase_two(3)
    gather_in.cross_own()
    gather_out.cross_own()
    phase_two(4)
    gather_in.pass_on()
    gather_out.pass_on()
    got = received(2)
    cell_id = lax.broadcasted_iota(jnp.int32, (n, n), 1).astype(F32)
    at_a = jnp.where(got[:, 256:257] == cell_id, 1.0, 0.0)
    at_b = jnp.where(got[:, 320:321] == cell_id, 1.0, 0.0)
    cell_weights = dot(at_a.T.astype(BF16), got[:, 0:128].astype(BF16)) + dot(
        at_b.T.astype(BF16), got[:, 128:256].astype(BF16)
    )

    middle = state + lon_inverse(3)
    mixed, mixed_inverse = normalise(middle)
    mixed_low = mixed.astype(BF16)
    gather_in.last()
    gather_out.last()

    units = ny * six

    def slope_of(co, g):
        block = win[co, g].reshape(units, FEATURES)
        slope_ref[co * nx + g] = gelu_parts(dot_t(mixed_low, block))[1]

    for g in gather_in.slabs():
        slope_of(core, g)
    for i, g in enumerate(gather_in.slabs()):
        arrive(("core", gather_in, i))
        slope_of(1 - core, g)
    tangent_middle = heading + lon_inverse(4)
    tangent_low = norm_linear(mixed, mixed_inverse, tangent_middle).astype(BF16)
    for i in range(ny):
        arrive(("core", gather_out, i))

    def tangent_step(i, total):
        co, t = lax.div(i, nx), lax.rem(i, nx)
        block_in = win[co, t].reshape(units, FEATURES)
        block_out = wout[co, :, t].reshape(units, FEATURES)
        hidden = (slope_ref[i] * dot_t(tangent_low, block_in)).astype(BF16)
        return total + dot(hidden, block_out)

    tangent_out = lax.fori_loop(0, 2 * nx, tangent_step, tangent_middle)

    load(readout_ref)
    readout = split(readout_ref[...])
    departures = dot_3(split(tangent_out), readout)
    gradient = dot_3(split(cell_weights * departures), readout, dot_t)
    gradient_low = gradient.astype(BF16)

    def grad_step(i, total):
        co, t = lax.div(i, nx), lax.rem(i, nx)
        block_in = win[co, t].reshape(units, FEATURES)
        block_out = wout[co, :, t].reshape(units, FEATURES)
        grad_pre = (slope_ref[i] * dot_t(gradient_low, block_out)).astype(BF16)
        return total + dot(grad_pre, block_in)

    grad_mixed = lax.fori_loop(0, 2 * nx, grad_step, jnp.zeros((n, FEATURES), F32))
    grad_middle = gradient + norm_linear(mixed, mixed_inverse, grad_mixed)

    lon_forward(5, grad_middle)
    phase_one(5)
    phase_two(5)
    lat_inverse(6, mix(spec_slope * mix(lat_forward(5), 1, dot_t), 0, dot_t))
    phase_one(6)
    phase_two(6)
    update = grad_middle + norm_linear(normed, inverse, lon_inverse(6))
    grad_ref[...] = update

    load(res_ref)
    residual = res_ref[...]
    hessian = heading + update
    sums = [
        jnp.sum(jnp.sum(v, axis=0, keepdims=True), axis=1, keepdims=True)
        for v in (residual * residual, heading * hessian, residual * hessian, hessian * hessian)
    ]
    place = lax.broadcasted_iota(jnp.int32, (1, 128), 1)
    total = jnp.zeros((1, 128), F32)
    for i, value in enumerate(sums):
        total = total + jnp.where(place == i, value, 0.0)

    def reduce_over(i, total, buffer, mine_at, partners, where):
        parts[i] = total
        for t in partners:
            push(parts.at[i], buffer.at[mine_at], rsems.at[i, 0], rsems.at[i, 1], where(t))
        pltpu.make_async_copy(parts.at[i], buffer.at[mine_at], rsems.at[i, 1]).start()
        leaving.append((buffer.at[pl.ds(0, len(partners))], rsems.at[i, 0]))
        wait_bytes(buffer, rsems.at[i, 1])
        return jnp.sum(buffer[...], axis=0)

    total = reduce_over(0, total, around, me_yc * nx + ens, plane, at_plane)
    total = reduce_over(1, total, along, zz, z_partners, at_z)
    norm_now, curvature, cross, square = total[:, 0:1], total[:, 1:2], total[:, 2:3], total[:, 3:4]
    step = norm_now / curvature
    norm_next = norm_now + step * (step * square - 2.0 * cross)
    ratio = norm_next / norm_now
    line = lax.broadcasted_iota(jnp.int32, (8, FEATURES), 0)
    scal_ref[...] = jnp.where(line == 0, step, ratio)
    finish()


def per_device(ny, nz, nx, background, increment, residual, direction, spec_in, spec_out, mlp_in,
               mlp_out, readout, obs_owner, obs_cell, obs_count, obs_weight):
    n = background.shape[2]
    group = 2 * ny
    six = 6 * nz
    narrow, wide, pack = make_tables(ny, nz)
    vmem = pl.BlockSpec(memory_space=pltpu.VMEM)
    operands = (
        background.reshape(n, FEATURES),
        jnp.asarray(narrow),
        direction.reshape(n, FEATURES),
        mlp_in.T,
        mlp_out,
        jnp.asarray(wide),
        spec_in.reshape(2, FEATURES, BLOCK),
        spec_out.reshape(2, FEATURES, BLOCK),
        jnp.asarray(pack),
        obs_owner.reshape(1, -1),
        obs_cell.reshape(1, -1),
        obs_count.reshape(1, 1),
        obs_weight,
        readout,
        residual.reshape(n, FEATURES),
    )
    update, scal = pl.pallas_call(
        functools.partial(kernel, ny, nz, nx),
        out_shape=(
            jax.ShapeDtypeStruct((n, FEATURES), F32),
            jax.ShapeDtypeStruct((8, FEATURES), F32),
        ),
        in_specs=[pl.BlockSpec(memory_space=pl.ANY)] * 15,
        out_specs=(vmem, vmem),
        scratch_shapes=[pltpu.VMEM(v.shape, v.dtype) for v in operands]
        + [
            pltpu.VMEM((FIELDS, group, nz, FEATURES), BF16),
            pltpu.VMEM((FIELDS, group, nz, FEATURES), BF16),
            pltpu.VMEM((FIELDS, nz, group, FEATURES), BF16),
            pltpu.VMEM((FIELDS, nz, group, FEATURES), BF16),
            pltpu.VMEM((min(4, nz), nz // min(4, nz), 16, FEATURES), BF16),
            pltpu.VMEM((2, nx, ny, six, FEATURES), BF16),
            pltpu.VMEM((2, ny, nx, six, FEATURES), BF16),
            pltpu.VMEM((2 * nx, n, ny * six), F32),
            pltpu.VMEM((4, FEATURES, FEATURES), BF16),
            pltpu.VMEM((group * nx, 1, 128), F32),
            pltpu.VMEM((nz, 1, 128), F32),
            pltpu.VMEM((2, 1, 128), F32),
            pltpu.SemaphoreType.DMA((FIELDS, 4)),
            pltpu.SemaphoreType.DMA((4,)),
            pltpu.SemaphoreType.DMA((2, 16)),
            pltpu.SemaphoreType.DMA((2, 2)),
            pltpu.SemaphoreType.DMA((15,)),
        ],
        compiler_params=pltpu.CompilerParams(
            collective_id=0, has_side_effects=True, vmem_limit_bytes=48 * 1024 * 1024
        ),
    )(*operands)
    step, ratio = scal[0:1], scal[1:2]
    hessian_dir = direction + update.reshape(direction.shape)
    residual_new = residual - step * hessian_dir
    return (
        increment + step * direction,
        residual_new,
        residual_new + ratio * direction,
        hessian_dir,
    )


def solution(mesh):
    n_lat, nx = mesh.shape["lat"], mesh.shape["ens"]
    nz = 16 if n_lat == 128 else 2
    ny = n_lat // (2 * nz)
    field = P("ens", "lat", None, None)
    return jax.shard_map(
        functools.partial(per_device, ny, nz, nx),
        mesh=mesh,
        in_specs=(
            field,
            field,
            field,
            field,
            P(),
            P(),
            P(None, ("lat", "ens")),
            P(("lat", "ens"), None),
            P(),
            P("lat", None),
            P("lat"),
            P("lat"),
            P("lat", None),
        ),
        out_specs=(field, field, field, field),
        check_vma=False,
    )
```

```python
import functools
import math

import jax
import jax.numpy as jnp
import numpy as np
from jax import lax
from jax.experimental import pallas as pl
from jax.experimental.pallas import tpu as pltpu
from jax.sharding import PartitionSpec as P

MESH = pl.DeviceIdType.MESH
F32 = jnp.float32
BF16 = jnp.bfloat16
NORM_EPSILON = 1e-05
FEATURES = 384
BLOCK = 48
FIELDS = 7
VMEM_BYTES = 63 * 1024 * 1024


def split_np(table):
    high = table.astype(np.float32).astype(jnp.bfloat16)
    low = (table - high.astype(np.float64)).astype(np.float32).astype(jnp.bfloat16)
    return high, low


def make_tables(ny, nz):
    chips = ny * nz
    n = 2 * chips
    scale = 1.0 / math.sqrt(n)
    pos = np.arange(n)
    angle = 2.0 * math.pi * ((pos[:, None] * pos[None, :]) % n) / n
    cosine, sine = np.cos(angle) * scale, np.sin(angle) * scale
    alternate = np.where(pos % 2 == 0, 1.0, -1.0) * scale
    lon_f = np.concatenate([cosine[:chips], -sine[:chips]], 0)
    lon_f[chips] = alternate
    y, z, a = np.meshgrid(np.arange(ny), np.arange(nz), np.arange(2), indexing="ij")
    row = (y * nz + z) * 2 + a
    arrive = row.transpose(1, 0, 2).reshape(-1)
    depart = row.transpose(0, 2, 1).reshape(-1)
    lat_f = np.concatenate([cosine[:, arrive], sine[:, arrive]], 1)
    lat_i = np.concatenate([cosine[depart], sine[depart]], 1)
    freq = (y * nz + z).transpose(1, 0, 2).reshape(-1)
    core = a.transpose(1, 0, 2).reshape(-1)
    imag = -sine[:, freq]
    imag[:, freq == 0] = alternate[:, None]
    lon_i = np.concatenate(
        [
            np.concatenate([np.where(core == b, cosine[:, freq], 0.0), np.where(core == b, imag, 0.0)], 1)
            for b in (0, 1)
        ],
        0,
    )
    group = 2 * ny
    perm = np.zeros((n, n))
    for s in range(group):
        for t in range(nz):
            perm[t * group + s, s * nz + t] = 1.0
    pack = np.zeros((12 * nz, 16 * nz))
    for t in range(nz):
        for u in range(6):
            pack[t * 6 + u, t * 16 + u] = 1.0
            pack[6 * nz + t * 6 + u, t * 16 + 8 + u] = 1.0
    narrow = np.concatenate([*split_np(lon_f), perm.astype(jnp.bfloat16)], 0)
    wide = np.concatenate([*split_np(lat_f), *split_np(lat_i), *split_np(lon_i)], 0)
    return narrow, wide, pack.astype(jnp.bfloat16)


def split(values):
    high = values.astype(BF16)
    return high, (values - high.astype(F32)).astype(BF16)


def dot(left, right):
    return jnp.dot(left, right, preferred_element_type=F32)


def dot_t(left, right):
    return lax.dot_general(left, right, (((1,), (1,)), ((), ())), preferred_element_type=F32)


def dot_3(left, right, op=dot):
    return op(left[0], right[0]) + (op(left[1], right[0]) + op(left[0], right[1]))


def normalise(values):
    centred = values - jnp.mean(values, axis=-1, keepdims=True)
    inverse = lax.rsqrt(jnp.mean(centred * centred, axis=-1, keepdims=True) + NORM_EPSILON)
    return centred * inverse, inverse


def norm_linear(normed, inverse, values):
    along = jnp.mean(normed * values, axis=-1, keepdims=True)
    return inverse * (values - jnp.mean(values, axis=-1, keepdims=True) - normed * along)


def gelu_parts(values):
    cumulative = 0.5 * (1.0 + lax.erf(values * (1.0 / math.sqrt(2.0))))
    density = jnp.exp(-0.5 * values * values) * (1.0 / math.sqrt(2.0 * math.pi))
    return values * cumulative, cumulative + values * density


def swap_parts(values):
    return jnp.concatenate(
        [values[:, 128:256], values[:, 0:128], pltpu.roll(values[:, 256:384], 64, 1)], axis=1
    )


def kernel(
    ny,
    nz,
    nx,
    *refs,
):
    inputs, (grad_ref, step_ref, ratio_ref), held, rest = refs[:15], refs[15:18], refs[18:33], refs[33:]
    (
        bg_ref,
        narrow_ref,
        dir_ref,
        mlp_in_ref,
        mlp_out_ref,
        wide_ref,
        spec_in_ref,
        spec_out_ref,
        pack_ref,
        owner_ref,
        cell_ref,
        count_ref,
        weight_ref,
        readout_ref,
        res_ref,
    ) = held
    (
        s1,
        r1,
        s2,
        r2,
        wz,
        win,
        wout,
        slope_ref,
        hidden,
        mixes,
        around,
        along,
        parts,
        sems,
        zsems,
        wsems,
        rsems,
        insems,
    ) = rest
    n = 2 * ny * nz
    chips = ny * nz
    group = 2 * ny
    lat = lax.axis_index("lat")
    ens = lax.axis_index("ens")
    core = lax.rem(lat, 2)
    chip = lax.div(lat, 2)
    yy = lax.div(chip, nz)
    zz = lax.rem(chip, nz)
    me_yc = yy * 2 + core

    def at_yc(k):
        return {"lat": (lax.div(k, 2) * nz + zz) * 2 + lax.rem(k, 2), "ens": ens}

    def at_z(t):
        return {"lat": (yy * nz + t) * 2 + core, "ens": ens}

    def at_x(t):
        return {"lat": lat, "ens": t}

    z_steps = sorted(range(1, nz), key=lambda s: (-min(s, nz - s), s))
    yc_partners = [lax.rem(me_yc + s, group) for s in range(1, group)]
    z_partners = [lax.rem(zz + s, nz) for s in z_steps]
    plane = [
        (lax.rem(me_yc + k, group), lax.rem(ens + t, nx))
        for k, t in sorted(
            ((k, t) for k in range(group) for t in range(nx) if k or t),
            key=lambda p: -min(p[0] // 2, ny - p[0] // 2) - min(p[1], nx - p[1]),
        )
    ]

    def at_plane(p):
        return {"lat": (lax.div(p[0], 2) * nz + zz) * 2 + lax.rem(p[0], 2), "ens": p[1]}

    for i in range(15):
        pltpu.make_async_copy(inputs[i], held[i], insems.at[i]).start()
    barrier = pltpu.get_barrier_semaphore()
    for t in z_partners:
        pl.semaphore_signal(barrier, inc=1, device_id=at_z(t), device_id_type=MESH)
    for p in plane:
        pl.semaphore_signal(barrier, inc=1, device_id=at_plane(p), device_id_type=MESH)

    ready = set()

    def load(*wanted):
        for ref in wanted:
            i = next(k for k in range(15) if held[k] is ref)
            if i not in ready:
                ready.add(i)
                pltpu.make_async_copy(inputs[i], ref, insems.at[i]).wait()

    leaving, coming = [], {}

    def push(source, target, send, recv, where):
        pltpu.make_async_remote_copy(
            src_ref=source,
            dst_ref=target,
            send_sem=send,
            recv_sem=recv,
            device_id=where,
            device_id_type=MESH,
        ).start()

    def wait_bytes(ref, sem):
        pltpu.make_async_copy(ref, ref, sem).wait()

    def arrive(key):
        wait_bytes(*coming.pop(key))

    def finish():
        load(*held)
        for key in list(coming):
            arrive(key)
        for ref, sem in leaving:
            wait_bytes(ref, sem)

    def phase_one(f):
        for k in yc_partners:
            push(s1.at[f, k], r1.at[f, me_yc], sems.at[f, 0], sems.at[f, 1], at_yc(k))
        pltpu.make_async_copy(s1.at[f, me_yc], r1.at[f, me_yc], sems.at[f, 1]).start()
        leaving.append((s1.at[f, pl.ds(0, group - 1)], sems.at[f, 0]))
        coming["one", f] = (r1.at[f], sems.at[f, 1])

    def phase_two(f):
        arrive(("one", f))
        turned = dot(narrow_ref[2 * n : 3 * n, :], r1[f].reshape(n, FEATURES))
        s2[f] = turned.reshape(nz, group, FEATURES).astype(BF16)
        for t in z_partners:
            push(s2.at[f, t], r2.at[f, zz], sems.at[f, 2], sems.at[f, 3], at_z(t))
        pltpu.make_async_copy(s2.at[f, zz], r2.at[f, zz], sems.at[f, 3]).start()
        leaving.append((s2.at[f, pl.ds(0, nz - 1)], sems.at[f, 2]))
        coming["two", f] = (r2.at[f], sems.at[f, 3])

    def received(f):
        arrive(("two", f))
        return r2[f].astype(F32).reshape(n, FEATURES)

    def lon_f():
        load(narrow_ref)
        return narrow_ref[0:n, :], narrow_ref[n : 2 * n, :]

    def lat_f():
        load(wide_ref)
        return wide_ref[0:n, :], wide_ref[n : 2 * n, :]

    def lat_i():
        return wide_ref[2 * n : 3 * n, :], wide_ref[3 * n : 4 * n, :]

    def lon_i():
        return wide_ref[4 * n : 6 * n, :], wide_ref[6 * n : 8 * n, :]

    lane = lax.broadcasted_iota(jnp.int32, (1, FEATURES), 1)
    low_half = lax.rem(lane, 128) < 64
    tail_real = low_half == (core == 0)
    mask_r = jnp.where(jnp.logical_or(lane < 128, jnp.logical_and(lane >= 256, tail_real)), 1.0, 0.0)
    mask_i = 1.0 - mask_r
    plain = jnp.where(chip == 0, 0.0, 1.0)
    first = 1.0 - plain
    low_lane = lax.broadcasted_iota(jnp.int32, (1, 128), 1) < 64

    def lon_forward(f, field):
        spectrum = dot_3(lon_f(), split(field))
        real, imag = spectrum[0:chips], spectrum[chips:n]
        imag_mid = pltpu.roll(imag[:, 128:256], 64, 1)
        real_mid = real[:, 128:256]
        for b in (0, 1):
            if b == 0:
                tiles = [real[:, 0:128], imag[:, 0:128], jnp.where(low_lane, real_mid, imag_mid)]
            else:
                tiles = [real[:, 256:384], imag[:, 256:384], jnp.where(low_lane, imag_mid, real_mid)]
            for i, tile in enumerate(tiles):
                low = tile.astype(BF16)
                for y in range(ny):
                    s1[f, 2 * y + b, :, i * 128 : (i + 1) * 128] = low[y * nz : (y + 1) * nz]

    def lon_inverse(f):
        values = received(f)
        tail = values[:, 256:384]
        stacked = jnp.concatenate(
            [
                jnp.concatenate([values[:, 0:128], tail], axis=1),
                jnp.concatenate([values[:, 128:256], pltpu.roll(tail, 64, 1)], axis=1),
            ],
            axis=0,
        ).astype(BF16)
        high, low = lon_i()
        out = dot(high, stacked) + dot(low, stacked)
        middle_tile = jnp.where(low_lane, out[0:n, 128:256], out[n : 2 * n, 128:256])
        return jnp.concatenate([out[0:n, 0:128], middle_tile, out[n : 2 * n, 0:128]], axis=1)

    def lat_forward(f):
        high, low = lat_f()
        x = received(f)
        sw = swap_parts(x)
        left = jnp.concatenate(
            [x * (mask_r + plain * mask_i), sw * (plain * mask_r - mask_i)], axis=0
        ).astype(BF16)
        right = jnp.concatenate(
            [
                x * (plain * mask_r - plain * mask_i) + sw * (first * mask_r),
                sw * (-plain) - x * (first * mask_i),
            ],
            axis=0,
        ).astype(BF16)
        return jnp.concatenate(
            [dot(high, left) + dot(low, left), dot(high, right) + dot(low, right)],
            axis=0,
        )

    def lat_inverse(f, both):
        a, b = both[0:n], both[n : 2 * n]
        sa, sb = swap_parts(a), swap_parts(b)
        upper = a * (mask_r + plain * mask_i) + b * (plain * (mask_r - mask_i)) + sb * (first * mask_i)
        lower = sa * (plain * mask_i - mask_r) - sb * plain - b * (first * mask_i)
        out = dot_3(lat_i(), split(jnp.concatenate([upper, lower], axis=0)))
        s1[f] = out.reshape(group, nz, FEATURES).astype(BF16)

    def mix(values, which, op=dot):
        return dot_3(split(values), (mixes[2 * which], mixes[2 * which + 1]), op)

    load(bg_ref)
    state = bg_ref[...].astype(F32)
    normed, inverse = normalise(state)
    lon_forward(0, normed)
    pick = lax.broadcasted_iota(jnp.int32, (16, 6), 0) - lax.broadcasted_iota(jnp.int32, (16, 6), 1)
    load(mlp_in_ref, mlp_out_ref)
    rows_in = dot(jnp.where(pick == 0, 1.0, 0.0).astype(BF16), mlp_in_ref[...])
    rows_out = dot(jnp.where(pick == 8, 1.0, 0.0).astype(BF16), mlp_out_ref[...])
    wz[lax.rem(zz, min(4, nz)), lax.div(zz, min(4, nz))] = (rows_in + rows_out).astype(BF16)
    load(dir_ref)
    heading = dir_ref[...]
    lon_forward(1, norm_linear(normed, inverse, heading))
    load(owner_ref, cell_ref, count_ref, weight_ref)
    rows = owner_ref.shape[1]
    owner_row = jnp.broadcast_to(owner_ref[...].astype(F32), (rows, rows))
    owner_col = owner_row.T
    cell_col = jnp.broadcast_to(cell_ref[...].astype(F32), (rows, rows)).T
    sub = lax.broadcasted_iota(jnp.int32, (rows, rows), 0)
    col = lax.broadcasted_iota(jnp.int32, (rows, rows), 1)
    again = jnp.where(jnp.logical_and(owner_col == owner_row, sub < col), 1.0, 0.0)
    rank = jnp.sum(again, axis=0, keepdims=True)
    slot = lax.broadcasted_iota(jnp.int32, (n, rows), 0)
    slot_k, slot_z = lax.div(slot, nz), lax.rem(slot, nz)
    slot_lat = (lax.div(slot_k, 2) * nz + slot_z) * 2 + lax.rem(slot_k, 2)
    mine = owner_row[0:1, :] == slot_lat.astype(F32)
    hit_a = jnp.where(jnp.logical_and(mine, rank == 0.0), 1.0, 0.0).astype(BF16)
    hit_b = jnp.where(jnp.logical_and(mine, rank == 1.0), 1.0, 0.0).astype(BF16)
    row_id = lax.broadcasted_iota(jnp.int32, weight_ref.shape, 0)
    weights = jnp.where(row_id < count_ref[...], weight_ref[...], 0.0).astype(BF16)
    cells = jnp.broadcast_to(cell_col[:, 0:1], (rows, 128)).astype(BF16)
    ids = jnp.where(low_lane, dot(hit_a, cells), dot(hit_b, cells))
    slots = jnp.concatenate([dot(hit_a, weights), dot(hit_b, weights), ids], axis=1)
    s1[2] = slots.reshape(group, nz, FEATURES).astype(BF16)
    pl.semaphore_wait(barrier, (nz - 1) + (group * nx - 1))
    phase_one(0)
    classes = min(4, nz)
    quads = nz // classes
    own_class, own_quad = lax.rem(zz, classes), lax.div(zz, classes)
    far = sorted(range(1, quads), key=lambda q: -min(q, quads - q))
    for q in far:
        target = lax.rem(zz + classes * q, nz)
        push(wz.at[own_class, own_quad], wz.at[own_class, own_quad], zsems.at[0], zsems.at[1], at_z(target))
    if far:
        leaving.append((wz.at[0, pl.ds(0, quads - 1)], zsems.at[0]))
        coming["quads"] = (wz.at[0, pl.ds(0, quads - 1)], zsems.at[1])
    phase_one(1)
    phase_one(2)
    phase_two(0)
    half = 4 * BLOCK
    p_row = lax.broadcasted_iota(jnp.int32, (FEATURES, 1), 0)

    def local_feature(p):
        within = lax.rem(p, 128)
        tail = lax.rem(p, 64)
        low_core = jnp.where(p < 256, within, 128 + tail)
        high_core = jnp.where(p < 256, 64 + within, tail)
        return jnp.where(core == 0, low_core, high_core)

    def block_of(u):
        return lax.div(u, BLOCK)

    row_tail_real = (lax.rem(p_row, 128) < 64) == (core == 0)
    row_real = jnp.logical_or(p_row < 128, jnp.logical_and(p_row >= 256, row_tail_real))
    u_row, u_lane = local_feature(p_row), local_feature(lane)
    spread = jnp.where(
        u_row == lax.broadcasted_iota(jnp.int32, (FEATURES, half), 1), 1.0, 0.0
    ).astype(BF16)
    widen = jnp.where(
        lax.broadcasted_iota(jnp.int32, (BLOCK, FEATURES), 0) == u_lane - BLOCK * block_of(u_lane), 1.0, 0.0
    ).astype(BF16)
    same_block = block_of(u_row) == block_of(u_lane)
    same_part = row_real == (mask_r > 0.5)
    cross_sign = jnp.where(row_real, 1.0, -1.0)
    load(spec_in_ref, spec_out_ref)
    for which, ref in ((0, spec_in_ref), (1, spec_out_ref)):
        real_pair = split(ref[0, pl.ds(core * half, half), :])
        imag_pair = split(ref[1, pl.ds(core * half, half), :])
        for level in (0, 1):
            real_part = dot(dot(spread, real_pair[level]).astype(BF16), widen)
            imag_part = dot(dot(spread, imag_pair[level]).astype(BF16), widen)
            dense = jnp.where(same_part, real_part, imag_part * cross_sign)
            mixes[2 * which + level] = jnp.where(same_block, dense, 0.0).astype(BF16)

    if far:
        arrive("quads")
    near = [1, nz - 1, 2][: classes - 1]
    for step in near:
        push(wz.at[own_class], wz.at[own_class], zsems.at[2], zsems.at[3], at_z(lax.rem(zz + step, nz)))
    if near:
        leaving.append((wz.at[pl.ds(0, classes - 1)], zsems.at[2]))
        coming["classes"] = (wz.at[pl.ds(0, classes - 1)], zsems.at[3])
    phase_two(1)
    six = 6 * nz
    sibling = at_yc(yy * 2 + (1 - core))

    class Gather:
        def __init__(self, ref, which, first, second, first_at, second_at, first_n, second_n):
            self.ref, self.sem, self.f, self.g = ref, lambda i: wsems.at[which, i], first, second
            self.which, self.first_at, self.second_at = which, first_at, second_at
            self.nf, self.ng = first_n, second_n
            self.left = lax.rem(second + second_n - 1, second_n)
            self.right = lax.rem(second + 1, second_n)
            self.order = sorted(range(first_n), key=lambda i: (min(i, first_n - i), i))

        def block(self, g, f):
            return self.ref.at[core, g, f] if self.which == 0 else self.ref.at[core, f, g]

        def slab(self, g):
            return self.ref.at[core, g] if self.which == 0 else self.ref.at[core, :, g]

        def blocks(self, count):
            part = pl.ds(0, count)
            return self.ref.at[0, 0, part] if self.which == 0 else self.ref.at[0, part, 0]

        def offset(self, i):
            return lax.rem(self.f + i, self.nf)

        def beside(self, i):
            mine = self.block(self.g, self.offset(i))
            if self.ng > 1:
                push(mine, mine, self.sem(4), self.sem(8 + i), self.second_at(self.right))
                coming["left", self, i] = (self.blocks(1), self.sem(8 + i))
            if self.ng > 2:
                push(mine, mine, self.sem(5), self.sem(12 + i), self.second_at(self.left))
                coming["right", self, i] = (self.blocks(1), self.sem(12 + i))

        def begin(self):
            mine = self.block(self.g, self.f)
            for i in self.order[1:]:
                push(mine, mine, self.sem(0), self.sem(self.nf - i), self.first_at(self.offset(i)))
                coming["first", self, self.nf - i] = (self.blocks(1), self.sem(self.nf - i))
            self.beside(0)
            if self.nf > 1:
                leaving.append((self.blocks(self.nf - 1), self.sem(0)))
            if self.ng > 1:
                leaving.append((self.blocks(self.nf), self.sem(4)))
            if self.ng > 2:
                leaving.append((self.blocks(self.nf), self.sem(5)))

        def spread(self, i):
            arrive(("first", self, i))
            self.beside(i)

        def cross(self, g, i):
            slab = self.slab(g)
            push(slab, slab, self.sem(16 + 2 * i), self.sem(17 + 2 * i), sibling)
            leaving.append((slab, self.sem(16 + 2 * i)))
            coming["core", self, i] = (slab, self.sem(17 + 2 * i))

        def pass_on(self, i):
            half = six // 2
            for key, origin, target, part in (
                ("left", self.left, self.right, pl.ds(0, half)),
                ("right", self.right, self.left, pl.ds(half, half)),
            ):
                if (key, self, i) in coming:
                    arrive((key, self, i))
                if self.ng > 2:
                    ref = self.block(origin, self.offset(i)).at[part]
                    push(ref, ref, self.sem(6), self.sem(7), self.second_at(target))
            if i == self.order[-1]:
                if self.ng > 2:
                    leaving.append((self.blocks(self.nf), self.sem(6)))
                    coming["opposite", self] = (self.blocks(self.nf), self.sem(7))
                if self.ng > 1:
                    self.cross(self.left, 1)
                if self.ng > 2:
                    self.cross(self.right, 2)

        def last(self):
            if self.ng > 2:
                arrive(("opposite", self))
                self.cross(lax.rem(self.g + 2, self.ng), 3)

        def slabs(self):
            return [self.g, self.left, self.right, lax.rem(self.g + 2, self.ng)][: self.ng]

    def at_y(t):
        return at_yc(t * 2 + core)

    gather_in = Gather(win, 0, yy, ens, at_y, at_x, ny, nx)
    gather_out = Gather(wout, 1, ens, yy, at_x, at_y, nx, ny)
    before = mix(lat_forward(0), 0)
    value, spec_slope = gelu_parts(before)
    lat_inverse(3, mix(value, 1))
    phase_one(3)
    if near:
        arrive("classes")
    load(pack_ref)
    packed = dot(pack_ref[...], wz[...].reshape(16 * nz, FEATURES)).astype(BF16)
    win[core, ens, yy] = packed[0:six]
    wout[core, ens, yy] = packed[six : 2 * six]
    gather_in.begin()
    gather_out.begin()
    phase_two(3)

    lat_inverse(4, mix(spec_slope * mix(lat_forward(1), 0), 1))
    phase_one(4)
    for i in range(1, max(nx, ny)):
        for gather in (gather_in, gather_out):
            if i < gather.nf:
                gather.spread(gather.order[i])
    phase_two(4)
    for gather in (gather_in, gather_out):
        gather.cross(gather.g, 0)
    phase_two(2)
    for i in range(max(nx, ny)):
        for gather in (gather_in, gather_out):
            if i < gather.nf:
                gather.pass_on(gather.order[i])

    middle = state + lon_inverse(3)
    mixed, mixed_inverse = normalise(middle)
    mixed_low = mixed.astype(BF16)

    units = ny * six

    def slope_of(co, g):
        block = win[co, g].reshape(units, FEATURES)
        slope_ref[co * nx + g] = gelu_parts(dot_t(mixed_low, block))[1]

    slabs = gather_in.slabs()
    slope_of(core, slabs[0])
    arrive(("core", gather_in, 0))
    slope_of(1 - core, slabs[0])
    for i in range(1, min(3, nx)):
        slope_of(core, slabs[i])
    got = received(2)
    cell_id = lax.broadcasted_iota(jnp.int32, (n, n), 1).astype(F32)
    at_a = jnp.where(got[:, 256:257] == cell_id, 1.0, 0.0)
    at_b = jnp.where(got[:, 320:321] == cell_id, 1.0, 0.0)
    cell_weights = dot(at_a.T.astype(BF16), got[:, 0:128].astype(BF16)) + dot(
        at_b.T.astype(BF16), got[:, 128:256].astype(BF16)
    )

    gather_in.last()
    gather_out.last()
    for i in range(1, nx):
        if i == 3:
            slope_of(core, slabs[i])
        arrive(("core", gather_in, i))
        slope_of(1 - core, slabs[i])
    tangent_middle = heading + lon_inverse(4)
    tangent_low = norm_linear(mixed, mixed_inverse, tangent_middle).astype(BF16)
    for i in range(ny):
        arrive(("core", gather_out, i))

    def through(values_low, ref):
        for i in range(2 * nx):
            block = ref[i // nx, i % nx].reshape(units, FEATURES)
            hidden[:, i * units : (i + 1) * units] = (slope_ref[i] * dot_t(values_low, block)).astype(BF16)
        return hidden[...]

    tangent_out = tangent_middle + dot(through(tangent_low, win), wout[...].reshape(-1, FEATURES))
    load(readout_ref)
    readout = split(readout_ref[...])
    departures = dot_3(split(tangent_out), readout)
    gradient = dot_3(split(cell_weights * departures), readout, dot_t)
    gradient_low = gradient.astype(BF16)

    grad_mixed = dot(through(gradient_low, wout), win[...].reshape(-1, FEATURES))
    grad_middle = gradient + norm_linear(mixed, mixed_inverse, grad_mixed)

    lon_forward(5, grad_middle)
    phase_one(5)
    phase_two(5)
    lat_inverse(6, mix(spec_slope * mix(lat_forward(5), 1, dot_t), 0, dot_t))
    phase_one(6)
    phase_two(6)
    update = grad_middle + norm_linear(normed, inverse, lon_inverse(6))
    grad_ref[...] = update

    load(res_ref)
    residual = res_ref[...]
    hessian = heading + update
    sums = [
        jnp.sum(jnp.sum(v, axis=0, keepdims=True), axis=1, keepdims=True)
        for v in (residual * residual, heading * hessian, residual * hessian, hessian * hessian)
    ]
    place = lax.broadcasted_iota(jnp.int32, (1, 128), 1)
    total = jnp.zeros((1, 128), F32)
    for i, value in enumerate(sums):
        total = total + jnp.where(place == i, value, 0.0)

    def reduce_over(i, total, buffer, mine_at, partners, where):
        parts[i] = total
        for t in partners:
            push(parts.at[i], buffer.at[mine_at], rsems.at[i, 0], rsems.at[i, 1], where(t))
        pltpu.make_async_copy(parts.at[i], buffer.at[mine_at], rsems.at[i, 1]).start()
        leaving.append((buffer.at[pl.ds(0, len(partners))], rsems.at[i, 0]))
        wait_bytes(buffer, rsems.at[i, 1])
        return jnp.sum(buffer[...], axis=0)

    total = reduce_over(0, total, around, me_yc * nx + ens, plane, at_plane)
    total = reduce_over(1, total, along, zz, z_partners, at_z)
    norm_now, curvature, cross, square = total[:, 0:1], total[:, 1:2], total[:, 2:3], total[:, 3:4]
    step = norm_now / curvature
    norm_next = norm_now + step * (step * square - 2.0 * cross)
    ratio = norm_next / norm_now
    step_ref[...] = jnp.broadcast_to(step, step_ref.shape)
    ratio_ref[...] = jnp.broadcast_to(ratio, ratio_ref.shape)
    finish()


def per_device(ny, nz, nx, background, increment, residual, direction, spec_in, spec_out, mlp_in,
               mlp_out, readout, obs_owner, obs_cell, obs_count, obs_weight):
    n = background.shape[2]
    group = 2 * ny
    six = 6 * nz
    narrow, wide, pack = make_tables(ny, nz)
    vmem = pl.BlockSpec(memory_space=pltpu.VMEM)
    operands = (
        background.reshape(n, FEATURES),
        jnp.asarray(narrow),
        direction.reshape(n, FEATURES),
        mlp_in.T,
        mlp_out,
        jnp.asarray(wide),
        spec_in.reshape(2, FEATURES, BLOCK),
        spec_out.reshape(2, FEATURES, BLOCK),
        jnp.asarray(pack),
        obs_owner.reshape(1, -1),
        obs_cell.reshape(1, -1),
        obs_count.reshape(1, 1),
        obs_weight,
        readout,
        residual.reshape(n, FEATURES),
    )
    update, step, ratio = pl.pallas_call(
        functools.partial(kernel, ny, nz, nx),
        out_shape=(
            jax.ShapeDtypeStruct((n, FEATURES), F32),
            jax.ShapeDtypeStruct((1, FEATURES), F32),
            jax.ShapeDtypeStruct((1, FEATURES), F32),
        ),
        in_specs=[pl.BlockSpec(memory_space=pl.ANY)] * 15,
        out_specs=(vmem, vmem, vmem),
        scratch_shapes=[pltpu.VMEM(v.shape, v.dtype) for v in operands]
        + [
            pltpu.VMEM((FIELDS, group, nz, FEATURES), BF16),
            pltpu.VMEM((FIELDS, group, nz, FEATURES), BF16),
            pltpu.VMEM((FIELDS, nz, group, FEATURES), BF16),
            pltpu.VMEM((FIELDS, nz, group, FEATURES), BF16),
            pltpu.VMEM((min(4, nz), nz // min(4, nz), 16, FEATURES), BF16),
            pltpu.VMEM((2, nx, ny, six, FEATURES), BF16),
            pltpu.VMEM((2, nx, ny, six, FEATURES), BF16),
            pltpu.VMEM((2 * nx, n, ny * six), F32),
            pltpu.VMEM((n, 2 * nx * ny * six), BF16),
            pltpu.VMEM((4, FEATURES, FEATURES), BF16),
            pltpu.VMEM((group * nx, 1, 128), F32),
            pltpu.VMEM((nz, 1, 128), F32),
            pltpu.VMEM((2, 1, 128), F32),
            pltpu.SemaphoreType.DMA((FIELDS, 4)),
            pltpu.SemaphoreType.DMA((4,)),
            pltpu.SemaphoreType.DMA((2, 24)),
            pltpu.SemaphoreType.DMA((2, 2)),
            pltpu.SemaphoreType.DMA((15,)),
        ],
        compiler_params=pltpu.CompilerParams(
            collective_id=0, has_side_effects=True, vmem_limit_bytes=VMEM_BYTES
        ),
    )(*operands)
    step, ratio = (v.reshape(1, 1, 1, FEATURES) for v in (step, ratio))
    hessian_dir = direction + update.reshape(direction.shape)
    residual_new = residual - step * hessian_dir
    return (
        increment + step * direction,
        residual_new,
        residual_new + ratio * direction,
        hessian_dir,
    )


def solution(mesh):
    n_lat, nx = mesh.shape["lat"], mesh.shape["ens"]
    nz = 16 if n_lat == 128 else 2
    ny = n_lat // (2 * nz)
    field = P("ens", "lat", None, None)
    return jax.shard_map(
        functools.partial(per_device, ny, nz, nx),
        mesh=mesh,
        in_specs=(
            field,
            field,
            field,
            field,
            P(),
            P(),
            P(None, ("lat", "ens")),
            P(("lat", "ens"), None),
            P(),
            P("lat", None),
            P("lat"),
            P("lat"),
            P("lat", None),
        ),
        out_specs=(field, field, field, field),
        check_vma=False,
    )
```

```python
import functools
import math

import jax
import jax.numpy as jnp
import numpy as np
from jax import lax
from jax.experimental import pallas as pl
from jax.experimental.pallas import tpu as pltpu
from jax.sharding import PartitionSpec as P

MESH = pl.DeviceIdType.MESH
F32 = jnp.float32
BF16 = jnp.bfloat16
NORM_EPSILON = 1e-05
FEATURES = 384
BLOCK = 48
FIELDS = 7
VMEM_BYTES = 63 * 1024 * 1024


def split_np(table):
    high = table.astype(np.float32).astype(jnp.bfloat16)
    low = (table - high.astype(np.float64)).astype(np.float32).astype(jnp.bfloat16)
    return high, low


def make_tables(ny, nz):
    chips = ny * nz
    n = 2 * chips
    scale = 1.0 / math.sqrt(n)
    pos = np.arange(n)
    angle = 2.0 * math.pi * ((pos[:, None] * pos[None, :]) % n) / n
    cosine, sine = np.cos(angle) * scale, np.sin(angle) * scale
    alternate = np.where(pos % 2 == 0, 1.0, -1.0) * scale
    lon_f = np.concatenate([cosine[:chips], -sine[:chips]], 0)
    lon_f[chips] = alternate
    y, z, a = np.meshgrid(np.arange(ny), np.arange(nz), np.arange(2), indexing="ij")
    row = (y * nz + z) * 2 + a
    arrive = row.transpose(1, 0, 2).reshape(-1)
    depart = row.transpose(0, 2, 1).reshape(-1)
    lat_f = np.concatenate([cosine[:, arrive], sine[:, arrive]], 1)
    lat_i = np.concatenate([cosine[depart], sine[depart]], 1)
    freq = (y * nz + z).transpose(1, 0, 2).reshape(-1)
    core = a.transpose(1, 0, 2).reshape(-1)
    imag = -sine[:, freq]
    imag[:, freq == 0] = alternate[:, None]
    lon_i = np.concatenate(
        [
            np.concatenate([np.where(core == b, cosine[:, freq], 0.0), np.where(core == b, imag, 0.0)], 1)
            for b in (0, 1)
        ],
        0,
    )
    group = 2 * ny
    perm = np.zeros((n, n))
    for s in range(group):
        for t in range(nz):
            perm[t * group + s, s * nz + t] = 1.0
    pack = np.zeros((12 * nz, 16 * nz))
    for t in range(nz):
        for u in range(6):
            pack[t * 6 + u, t * 16 + u] = 1.0
            pack[6 * nz + t * 6 + u, t * 16 + 8 + u] = 1.0
    narrow = np.concatenate([*split_np(lon_f), perm.astype(jnp.bfloat16)], 0)
    wide = np.concatenate([*split_np(lat_f), *split_np(lat_i), *split_np(lon_i)], 0)
    return narrow, wide, pack.astype(jnp.bfloat16)


def split(values):
    high = values.astype(BF16)
    return high, (values - high.astype(F32)).astype(BF16)


def dot(left, right):
    return jnp.dot(left, right, preferred_element_type=F32)


def dot_t(left, right):
    return lax.dot_general(left, right, (((1,), (1,)), ((), ())), preferred_element_type=F32)


def dot_3(left, right, op=dot):
    return op(left[0], right[0]) + (op(left[1], right[0]) + op(left[0], right[1]))


def normalise(values):
    centred = values - jnp.mean(values, axis=-1, keepdims=True)
    inverse = lax.rsqrt(jnp.mean(centred * centred, axis=-1, keepdims=True) + NORM_EPSILON)
    return centred * inverse, inverse


def norm_linear(normed, inverse, values):
    along = jnp.mean(normed * values, axis=-1, keepdims=True)
    return inverse * (values - jnp.mean(values, axis=-1, keepdims=True) - normed * along)


def gelu_parts(values):
    cumulative = 0.5 * (1.0 + lax.erf(values * (1.0 / math.sqrt(2.0))))
    density = jnp.exp(-0.5 * values * values) * (1.0 / math.sqrt(2.0 * math.pi))
    return values * cumulative, cumulative + values * density


def swap_parts(values):
    return jnp.concatenate(
        [values[:, 128:256], values[:, 0:128], pltpu.roll(values[:, 256:384], 64, 1)], axis=1
    )


def kernel(
    ny,
    nz,
    nx,
    *refs,
):
    inputs, (grad_ref, step_ref, ratio_ref), held, rest = refs[:15], refs[15:18], refs[18:33], refs[33:]
    (
        bg_ref,
        narrow_ref,
        dir_ref,
        mlp_in_ref,
        mlp_out_ref,
        wide_ref,
        spec_in_ref,
        spec_out_ref,
        pack_ref,
        owner_ref,
        cell_ref,
        count_ref,
        weight_ref,
        readout_ref,
        res_ref,
    ) = held
    (
        s1,
        r1,
        s2,
        r2,
        wz,
        win,
        wout,
        slope_ref,
        hidden,
        mixes,
        around,
        along,
        parts,
        sems,
        zsems,
        wsems,
        rsems,
        insems,
    ) = rest
    n = 2 * ny * nz
    chips = ny * nz
    group = 2 * ny
    lat = lax.axis_index("lat")
    ens = lax.axis_index("ens")
    core = lax.rem(lat, 2)
    chip = lax.div(lat, 2)
    yy = lax.div(chip, nz)
    zz = lax.rem(chip, nz)
    me_yc = yy * 2 + core

    def at_yc(k):
        return {"lat": (lax.div(k, 2) * nz + zz) * 2 + lax.rem(k, 2), "ens": ens}

    def at_z(t):
        return {"lat": (yy * nz + t) * 2 + core, "ens": ens}

    def at_x(t):
        return {"lat": lat, "ens": t}

    z_steps = sorted(range(1, nz), key=lambda s: (-min(s, nz - s), s))
    yc_partners = [
        lax.rem(yy + d, ny) * 2 + lax.rem(core + c, 2)
        for d, c in sorted(
            ((d, c) for d in range(ny) for c in (0, 1) if d or c), key=lambda p: -min(p[0], ny - p[0])
        )
    ]
    z_partners = [lax.rem(zz + s, nz) for s in z_steps]
    plane = [
        (lax.rem(me_yc + k, group), lax.rem(ens + t, nx))
        for k, t in sorted(
            ((k, t) for k in range(group) for t in range(nx) if k or t),
            key=lambda p: -min(p[0] // 2, ny - p[0] // 2) - min(p[1], nx - p[1]),
        )
    ]

    def at_plane(p):
        return {"lat": (lax.div(p[0], 2) * nz + zz) * 2 + lax.rem(p[0], 2), "ens": p[1]}

    for i in range(15):
        pltpu.make_async_copy(inputs[i], held[i], insems.at[i]).start()
    barrier = pltpu.get_barrier_semaphore()
    for t in z_partners:
        pl.semaphore_signal(barrier, inc=1, device_id=at_z(t), device_id_type=MESH)
    for p in plane:
        pl.semaphore_signal(barrier, inc=1, device_id=at_plane(p), device_id_type=MESH)

    ready = set()

    def load(*wanted):
        for ref in wanted:
            i = next(k for k in range(15) if held[k] is ref)
            if i not in ready:
                ready.add(i)
                pltpu.make_async_copy(inputs[i], ref, insems.at[i]).wait()

    leaving, coming = [], {}

    def push(source, target, send, recv, where):
        pltpu.make_async_remote_copy(
            src_ref=source,
            dst_ref=target,
            send_sem=send,
            recv_sem=recv,
            device_id=where,
            device_id_type=MESH,
        ).start()

    def wait_bytes(ref, sem):
        pltpu.make_async_copy(ref, ref, sem).wait()

    def arrive(key):
        wait_bytes(*coming.pop(key))

    def finish():
        load(*held)
        for key in list(coming):
            arrive(key)
        for ref, sem in leaving:
            wait_bytes(ref, sem)

    def phase_one(f):
        for k in yc_partners:
            push(s1.at[f, k], r1.at[f, me_yc], sems.at[f, 0], sems.at[f, 1], at_yc(k))
        pltpu.make_async_copy(s1.at[f, me_yc], r1.at[f, me_yc], sems.at[f, 1]).start()
        leaving.append((s1.at[f, pl.ds(0, group - 1)], sems.at[f, 0]))
        coming["one", f] = (r1.at[f], sems.at[f, 1])

    def phase_two(f):
        arrive(("one", f))
        turned = dot(narrow_ref[2 * n : 3 * n, :], r1[f].reshape(n, FEATURES))
        s2[f] = turned.reshape(nz, group, FEATURES).astype(BF16)
        for t in z_partners:
            push(s2.at[f, t], r2.at[f, zz], sems.at[f, 2], sems.at[f, 3], at_z(t))
        pltpu.make_async_copy(s2.at[f, zz], r2.at[f, zz], sems.at[f, 3]).start()
        leaving.append((s2.at[f, pl.ds(0, nz - 1)], sems.at[f, 2]))
        coming["two", f] = (r2.at[f], sems.at[f, 3])

    def received(f):
        arrive(("two", f))
        return r2[f].astype(F32).reshape(n, FEATURES)

    def lon_f():
        load(narrow_ref)
        return narrow_ref[0:n, :], narrow_ref[n : 2 * n, :]

    def lat_f():
        load(wide_ref)
        return wide_ref[0:n, :], wide_ref[n : 2 * n, :]

    def lat_i():
        return wide_ref[2 * n : 3 * n, :], wide_ref[3 * n : 4 * n, :]

    def lon_i():
        return wide_ref[4 * n : 6 * n, :], wide_ref[6 * n : 8 * n, :]

    lane = lax.broadcasted_iota(jnp.int32, (1, FEATURES), 1)
    low_half = lax.rem(lane, 128) < 64
    tail_real = low_half == (core == 0)
    mask_r = jnp.where(jnp.logical_or(lane < 128, jnp.logical_and(lane >= 256, tail_real)), 1.0, 0.0)
    mask_i = 1.0 - mask_r
    plain = jnp.where(chip == 0, 0.0, 1.0)
    first = 1.0 - plain
    low_lane = lax.broadcasted_iota(jnp.int32, (1, 128), 1) < 64

    def lon_forward(f, field):
        spectrum = dot_3(lon_f(), split(field))
        real, imag = spectrum[0:chips], spectrum[chips:n]
        imag_mid = pltpu.roll(imag[:, 128:256], 64, 1)
        real_mid = real[:, 128:256]
        for b in (0, 1):
            if b == 0:
                tiles = [real[:, 0:128], imag[:, 0:128], jnp.where(low_lane, real_mid, imag_mid)]
            else:
                tiles = [real[:, 256:384], imag[:, 256:384], jnp.where(low_lane, imag_mid, real_mid)]
            for i, tile in enumerate(tiles):
                low = tile.astype(BF16)
                for y in range(ny):
                    s1[f, 2 * y + b, :, i * 128 : (i + 1) * 128] = low[y * nz : (y + 1) * nz]

    def lon_inverse(f):
        values = received(f)
        tail = values[:, 256:384]
        stacked = jnp.concatenate(
            [
                jnp.concatenate([values[:, 0:128], tail], axis=1),
                jnp.concatenate([values[:, 128:256], pltpu.roll(tail, 64, 1)], axis=1),
            ],
            axis=0,
        ).astype(BF16)
        high, low = lon_i()
        out = dot(high, stacked) + dot(low, stacked)
        middle_tile = jnp.where(low_lane, out[0:n, 128:256], out[n : 2 * n, 128:256])
        return jnp.concatenate([out[0:n, 0:128], middle_tile, out[n : 2 * n, 0:128]], axis=1)

    def lat_forward(f):
        high, low = lat_f()
        x = received(f)
        sw = swap_parts(x)
        left = jnp.concatenate(
            [x * (mask_r + plain * mask_i), sw * (plain * mask_r - mask_i)], axis=0
        ).astype(BF16)
        right = jnp.concatenate(
            [
                x * (plain * mask_r - plain * mask_i) + sw * (first * mask_r),
                sw * (-plain) - x * (first * mask_i),
            ],
            axis=0,
        ).astype(BF16)
        return jnp.concatenate(
            [dot(high, left) + dot(low, left), dot(high, right) + dot(low, right)],
            axis=0,
        )

    def lat_inverse(f, both):
        a, b = both[0:n], both[n : 2 * n]
        sa, sb = swap_parts(a), swap_parts(b)
        upper = a * (mask_r + plain * mask_i) + b * (plain * (mask_r - mask_i)) + sb * (first * mask_i)
        lower = sa * (plain * mask_i - mask_r) - sb * plain - b * (first * mask_i)
        out = dot_3(lat_i(), split(jnp.concatenate([upper, lower], axis=0)))
        s1[f] = out.reshape(group, nz, FEATURES).astype(BF16)

    def mix(values, which, op=dot):
        return dot_3(split(values), (mixes[2 * which], mixes[2 * which + 1]), op)

    load(bg_ref)
    state = bg_ref[...].astype(F32)
    normed, inverse = normalise(state)
    lon_forward(0, normed)
    pick = lax.broadcasted_iota(jnp.int32, (16, 6), 0) - lax.broadcasted_iota(jnp.int32, (16, 6), 1)
    load(mlp_in_ref, mlp_out_ref)
    rows_in = dot(jnp.where(pick == 0, 1.0, 0.0).astype(BF16), mlp_in_ref[...])
    rows_out = dot(jnp.where(pick == 8, 1.0, 0.0).astype(BF16), mlp_out_ref[...])
    wz[lax.rem(zz, min(4, nz)), lax.div(zz, min(4, nz))] = (rows_in + rows_out).astype(BF16)
    load(dir_ref)
    heading = dir_ref[...]
    lon_forward(1, norm_linear(normed, inverse, heading))
    load(owner_ref, cell_ref, count_ref, weight_ref)
    rows = owner_ref.shape[1]
    owner_row = jnp.broadcast_to(owner_ref[...].astype(F32), (rows, rows))
    owner_col = owner_row.T
    cell_col = jnp.broadcast_to(cell_ref[...].astype(F32), (rows, rows)).T
    sub = lax.broadcasted_iota(jnp.int32, (rows, rows), 0)
    col = lax.broadcasted_iota(jnp.int32, (rows, rows), 1)
    again = jnp.where(jnp.logical_and(owner_col == owner_row, sub < col), 1.0, 0.0)
    rank = jnp.sum(again, axis=0, keepdims=True)
    slot = lax.broadcasted_iota(jnp.int32, (n, rows), 0)
    slot_k, slot_z = lax.div(slot, nz), lax.rem(slot, nz)
    slot_lat = (lax.div(slot_k, 2) * nz + slot_z) * 2 + lax.rem(slot_k, 2)
    mine = owner_row[0:1, :] == slot_lat.astype(F32)
    hit_a = jnp.where(jnp.logical_and(mine, rank == 0.0), 1.0, 0.0).astype(BF16)
    hit_b = jnp.where(jnp.logical_and(mine, rank == 1.0), 1.0, 0.0).astype(BF16)
    row_id = lax.broadcasted_iota(jnp.int32, weight_ref.shape, 0)
    weights = jnp.where(row_id < count_ref[...], weight_ref[...], 0.0).astype(BF16)
    cells = jnp.broadcast_to(cell_col[:, 0:1], (rows, 128)).astype(BF16)
    ids = jnp.where(low_lane, dot(hit_a, cells), dot(hit_b, cells))
    slots = jnp.concatenate([dot(hit_a, weights), dot(hit_b, weights), ids], axis=1)
    s1[2] = slots.reshape(group, nz, FEATURES).astype(BF16)
    pl.semaphore_wait(barrier, (nz - 1) + (group * nx - 1))
    phase_one(0)
    classes = min(4, nz)
    quads = nz // classes
    own_class, own_quad = lax.rem(zz, classes), lax.div(zz, classes)
    far = sorted(range(1, quads), key=lambda q: -min(q, quads - q))
    for q in far:
        target = lax.rem(zz + classes * q, nz)
        push(wz.at[own_class, own_quad], wz.at[own_class, own_quad], zsems.at[0], zsems.at[1], at_z(target))
    if far:
        leaving.append((wz.at[0, pl.ds(0, quads - 1)], zsems.at[0]))
        coming["quads"] = (wz.at[0, pl.ds(0, quads - 1)], zsems.at[1])
    phase_one(1)
    phase_one(2)
    phase_two(0)
    half = 4 * BLOCK
    p_row = lax.broadcasted_iota(jnp.int32, (FEATURES, 1), 0)

    def local_feature(p):
        within = lax.rem(p, 128)
        tail = lax.rem(p, 64)
        low_core = jnp.where(p < 256, within, 128 + tail)
        high_core = jnp.where(p < 256, 64 + within, tail)
        return jnp.where(core == 0, low_core, high_core)

    def block_of(u):
        return lax.div(u, BLOCK)

    row_tail_real = (lax.rem(p_row, 128) < 64) == (core == 0)
    row_real = jnp.logical_or(p_row < 128, jnp.logical_and(p_row >= 256, row_tail_real))
    u_row, u_lane = local_feature(p_row), local_feature(lane)
    spread = jnp.where(
        u_row == lax.broadcasted_iota(jnp.int32, (FEATURES, half), 1), 1.0, 0.0
    ).astype(BF16)
    widen = jnp.where(
        lax.broadcasted_iota(jnp.int32, (BLOCK, FEATURES), 0) == u_lane - BLOCK * block_of(u_lane), 1.0, 0.0
    ).astype(BF16)
    same_block = block_of(u_row) == block_of(u_lane)
    same_part = row_real == (mask_r > 0.5)
    cross_sign = jnp.where(row_real, 1.0, -1.0)
    load(spec_in_ref, spec_out_ref)
    for which, ref in ((0, spec_in_ref), (1, spec_out_ref)):
        real_pair = split(ref[0, pl.ds(core * half, half), :])
        imag_pair = split(ref[1, pl.ds(core * half, half), :])
        for level in (0, 1):
            real_part = dot(dot(spread, real_pair[level]).astype(BF16), widen)
            imag_part = dot(dot(spread, imag_pair[level]).astype(BF16), widen)
            dense = jnp.where(same_part, real_part, imag_part * cross_sign)
            mixes[2 * which + level] = jnp.where(same_block, dense, 0.0).astype(BF16)

    if far:
        arrive("quads")
    near = [1, nz - 1, 2][: classes - 1]
    for step in near:
        push(wz.at[own_class], wz.at[own_class], zsems.at[2], zsems.at[3], at_z(lax.rem(zz + step, nz)))
    if near:
        leaving.append((wz.at[pl.ds(0, classes - 1)], zsems.at[2]))
        coming["classes"] = (wz.at[pl.ds(0, classes - 1)], zsems.at[3])
    phase_two(1)
    six = 6 * nz
    sibling = at_yc(yy * 2 + (1 - core))

    class Gather:
        def __init__(self, ref, which, first, second, first_at, second_at, first_n, second_n):
            self.ref, self.sem, self.f, self.g = ref, lambda i: wsems.at[which, i], first, second
            self.which, self.first_at, self.second_at = which, first_at, second_at
            self.nf, self.ng = first_n, second_n
            self.left = lax.rem(second + second_n - 1, second_n)
            self.right = lax.rem(second + 1, second_n)
            self.order = sorted(range(first_n), key=lambda i: (min(i, first_n - i), i))

        def block(self, g, f):
            return self.ref.at[core, g, f] if self.which == 0 else self.ref.at[core, f, g]

        def slab(self, g):
            return self.ref.at[core, g] if self.which == 0 else self.ref.at[core, :, g]

        def blocks(self, count):
            part = pl.ds(0, count)
            return self.ref.at[0, 0, part] if self.which == 0 else self.ref.at[0, part, 0]

        def offset(self, i):
            return lax.rem(self.f + i, self.nf)

        def beside(self, i):
            mine = self.block(self.g, self.offset(i))
            if self.ng > 1:
                push(mine, mine, self.sem(4), self.sem(8 + i), self.second_at(self.right))
                coming["left", self, i] = (self.blocks(1), self.sem(8 + i))
            if self.ng > 2:
                push(mine, mine, self.sem(5), self.sem(12 + i), self.second_at(self.left))
                coming["right", self, i] = (self.blocks(1), self.sem(12 + i))

        def begin(self):
            mine = self.block(self.g, self.f)
            for i in self.order[1:]:
                push(mine, mine, self.sem(0), self.sem(self.nf - i), self.first_at(self.offset(i)))
                coming["first", self, self.nf - i] = (self.blocks(1), self.sem(self.nf - i))
            self.beside(0)
            if self.nf > 1:
                leaving.append((self.blocks(self.nf - 1), self.sem(0)))
            if self.ng > 1:
                leaving.append((self.blocks(self.nf), self.sem(4)))
            if self.ng > 2:
                leaving.append((self.blocks(self.nf), self.sem(5)))

        def spread(self, i):
            arrive(("first", self, i))
            self.beside(i)

        def cross(self, g, i):
            slab = self.slab(g)
            push(slab, slab, self.sem(16 + 2 * i), self.sem(17 + 2 * i), sibling)
            leaving.append((slab, self.sem(16 + 2 * i)))
            coming["core", self, i] = (slab, self.sem(17 + 2 * i))

        def pass_on(self, i):
            half = six // 2
            for key, origin, target, part in (
                ("left", self.left, self.right, pl.ds(0, half)),
                ("right", self.right, self.left, pl.ds(half, half)),
            ):
                if (key, self, i) in coming:
                    arrive((key, self, i))
                if self.ng > 2:
                    ref = self.block(origin, self.offset(i)).at[part]
                    push(ref, ref, self.sem(6), self.sem(7), self.second_at(target))
            if i == self.order[-1]:
                if self.ng > 2:
                    leaving.append((self.blocks(self.nf), self.sem(6)))
                    coming["opposite", self] = (self.blocks(self.nf), self.sem(7))
                if self.ng > 1:
                    self.cross(self.left, 1)
                if self.ng > 2:
                    self.cross(self.right, 2)

        def last(self):
            if self.ng > 2:
                arrive(("opposite", self))
                self.cross(lax.rem(self.g + 2, self.ng), 3)

        def slabs(self):
            return [self.g, self.left, self.right, lax.rem(self.g + 2, self.ng)][: self.ng]

    def at_y(t):
        return at_yc(t * 2 + core)

    gather_in = Gather(win, 0, yy, ens, at_y, at_x, ny, nx)
    gather_out = Gather(wout, 1, ens, yy, at_x, at_y, nx, ny)
    before = mix(lat_forward(0), 0)
    value, spec_slope = gelu_parts(before)
    lat_inverse(3, mix(value, 1))
    phase_one(3)
    if near:
        arrive("classes")
    load(pack_ref)
    packed = dot(pack_ref[...], wz[...].reshape(16 * nz, FEATURES)).astype(BF16)
    win[core, ens, yy] = packed[0:six]
    wout[core, ens, yy] = packed[six : 2 * six]
    gather_in.begin()
    gather_out.begin()
    phase_two(2)
    phase_two(3)

    lat_inverse(4, mix(spec_slope * mix(lat_forward(1), 0), 1))
    phase_one(4)
    for i in range(1, max(nx, ny)):
        for gather in (gather_in, gather_out):
            if i < gather.nf:
                gather.spread(gather.order[i])
    phase_two(4)
    for gather in (gather_in, gather_out):
        gather.cross(gather.g, 0)
    got = received(2)
    cell_id = lax.broadcasted_iota(jnp.int32, (n, n), 1).astype(F32)
    at_a = jnp.where(got[:, 256:257] == cell_id, 1.0, 0.0)
    at_b = jnp.where(got[:, 320:321] == cell_id, 1.0, 0.0)
    cell_weights = dot(at_a.T.astype(BF16), got[:, 0:128].astype(BF16)) + dot(
        at_b.T.astype(BF16), got[:, 128:256].astype(BF16)
    )

    for i in range(max(nx, ny)):
        for gather in (gather_in, gather_out):
            if i < gather.nf:
                gather.pass_on(gather.order[i])

    middle = state + lon_inverse(3)
    mixed, mixed_inverse = normalise(middle)
    mixed_low = mixed.astype(BF16)

    units = ny * six

    def slope_of(co, g):
        block = win[co, g].reshape(units, FEATURES)
        slope_ref[co * nx + g] = gelu_parts(dot_t(mixed_low, block))[1]

    slabs = gather_in.slabs()
    slope_of(core, slabs[0])
    arrive(("core", gather_in, 0))
    slope_of(1 - core, slabs[0])
    for i in range(1, min(3, nx)):
        slope_of(core, slabs[i])
    tangent_middle = heading + lon_inverse(4)
    tangent_low = norm_linear(mixed, mixed_inverse, tangent_middle).astype(BF16)
    gather_in.last()
    gather_out.last()
    for i in range(1, nx):
        if i == 3:
            slope_of(core, slabs[i])
        arrive(("core", gather_in, i))
        slope_of(1 - core, slabs[i])
    for i in range(ny):
        arrive(("core", gather_out, i))

    def through(values_low, ref):
        for i in range(2 * nx):
            block = ref[i // nx, i % nx].reshape(units, FEATURES)
            hidden[:, i * units : (i + 1) * units] = (slope_ref[i] * dot_t(values_low, block)).astype(BF16)
        return hidden[...]

    tangent_out = tangent_middle + dot(through(tangent_low, win), wout[...].reshape(-1, FEATURES))
    load(readout_ref)
    readout = split(readout_ref[...])
    departures = dot_3(split(tangent_out), readout)
    gradient = dot_3(split(cell_weights * departures), readout, dot_t)
    gradient_low = gradient.astype(BF16)

    grad_mixed = dot(through(gradient_low, wout), win[...].reshape(-1, FEATURES))
    grad_middle = gradient + norm_linear(mixed, mixed_inverse, grad_mixed)

    lon_forward(5, grad_middle)
    phase_one(5)
    phase_two(5)
    lat_inverse(6, mix(spec_slope * mix(lat_forward(5), 1, dot_t), 0, dot_t))
    phase_one(6)
    phase_two(6)
    update = grad_middle + norm_linear(normed, inverse, lon_inverse(6))
    grad_ref[...] = update

    load(res_ref)
    residual = res_ref[...]
    hessian = heading + update
    sums = [
        jnp.sum(jnp.sum(v, axis=0, keepdims=True), axis=1, keepdims=True)
        for v in (residual * residual, heading * hessian, residual * hessian, hessian * hessian)
    ]
    place = lax.broadcasted_iota(jnp.int32, (1, 128), 1)
    total = jnp.zeros((1, 128), F32)
    for i, value in enumerate(sums):
        total = total + jnp.where(place == i, value, 0.0)

    def reduce_over(i, total, buffer, mine_at, partners, where):
        parts[i] = total
        for t in partners:
            push(parts.at[i], buffer.at[mine_at], rsems.at[i, 0], rsems.at[i, 1], where(t))
        pltpu.make_async_copy(parts.at[i], buffer.at[mine_at], rsems.at[i, 1]).start()
        leaving.append((buffer.at[pl.ds(0, len(partners))], rsems.at[i, 0]))
        wait_bytes(buffer, rsems.at[i, 1])
        return jnp.sum(buffer[...], axis=0)

    total = reduce_over(0, total, around, me_yc * nx + ens, plane, at_plane)
    total = reduce_over(1, total, along, zz, z_partners, at_z)
    norm_now, curvature, cross, square = total[:, 0:1], total[:, 1:2], total[:, 2:3], total[:, 3:4]
    step = norm_now / curvature
    norm_next = norm_now + step * (step * square - 2.0 * cross)
    ratio = norm_next / norm_now
    step_ref[...] = jnp.broadcast_to(step, step_ref.shape)
    ratio_ref[...] = jnp.broadcast_to(ratio, ratio_ref.shape)
    finish()


def per_device(ny, nz, nx, background, increment, residual, direction, spec_in, spec_out, mlp_in,
               mlp_out, readout, obs_owner, obs_cell, obs_count, obs_weight):
    n = background.shape[2]
    group = 2 * ny
    six = 6 * nz
    narrow, wide, pack = make_tables(ny, nz)
    vmem = pl.BlockSpec(memory_space=pltpu.VMEM)
    operands = (
        background.reshape(n, FEATURES),
        jnp.asarray(narrow),
        direction.reshape(n, FEATURES),
        mlp_in.T,
        mlp_out,
        jnp.asarray(wide),
        spec_in.reshape(2, FEATURES, BLOCK),
        spec_out.reshape(2, FEATURES, BLOCK),
        jnp.asarray(pack),
        obs_owner.reshape(1, -1),
        obs_cell.reshape(1, -1),
        obs_count.reshape(1, 1),
        obs_weight,
        readout,
        residual.reshape(n, FEATURES),
    )
    update, step, ratio = pl.pallas_call(
        functools.partial(kernel, ny, nz, nx),
        out_shape=(
            jax.ShapeDtypeStruct((n, FEATURES), F32),
            jax.ShapeDtypeStruct((n, FEATURES), F32),
            jax.ShapeDtypeStruct((n, FEATURES), F32),
        ),
        in_specs=[pl.BlockSpec(memory_space=pl.ANY)] * 15,
        out_specs=(vmem, vmem, vmem),
        scratch_shapes=[pltpu.VMEM(v.shape, v.dtype) for v in operands]
        + [
            pltpu.VMEM((FIELDS, group, nz, FEATURES), BF16),
            pltpu.VMEM((FIELDS, group, nz, FEATURES), BF16),
            pltpu.VMEM((FIELDS, nz, group, FEATURES), BF16),
            pltpu.VMEM((FIELDS, nz, group, FEATURES), BF16),
            pltpu.VMEM((min(4, nz), nz // min(4, nz), 16, FEATURES), BF16),
            pltpu.VMEM((2, nx, ny, six, FEATURES), BF16),
            pltpu.VMEM((2, nx, ny, six, FEATURES), BF16),
            pltpu.VMEM((2 * nx, n, ny * six), F32),
            pltpu.VMEM((n, 2 * nx * ny * six), BF16),
            pltpu.VMEM((4, FEATURES, FEATURES), BF16),
            pltpu.VMEM((group * nx, 1, 128), F32),
            pltpu.VMEM((nz, 1, 128), F32),
            pltpu.VMEM((2, 1, 128), F32),
            pltpu.SemaphoreType.DMA((FIELDS, 4)),
            pltpu.SemaphoreType.DMA((4,)),
            pltpu.SemaphoreType.DMA((2, 24)),
            pltpu.SemaphoreType.DMA((2, 2)),
            pltpu.SemaphoreType.DMA((15,)),
        ],
        compiler_params=pltpu.CompilerParams(
            collective_id=0, has_side_effects=True, vmem_limit_bytes=VMEM_BYTES
        ),
    )(*operands)
    step, ratio = (v.reshape(direction.shape) for v in (step, ratio))
    hessian_dir = direction + update.reshape(direction.shape)
    residual_new = residual - step * hessian_dir
    return (
        increment + step * direction,
        residual_new,
        residual_new + ratio * direction,
        hessian_dir,
    )


def solution(mesh):
    n_lat, nx = mesh.shape["lat"], mesh.shape["ens"]
    nz = 16 if n_lat == 128 else 2
    ny = n_lat // (2 * nz)
    field = P("ens", "lat", None, None)
    return jax.shard_map(
        functools.partial(per_device, ny, nz, nx),
        mesh=mesh,
        in_specs=(
            field,
            field,
            field,
            field,
            P(),
            P(),
            P(None, ("lat", "ens")),
            P(("lat", "ens"), None),
            P(),
            P("lat", None),
            P("lat"),
            P("lat"),
            P("lat", None),
        ),
        out_specs=(field, field, field, field),
        check_vma=False,
    )
```

```python
import functools
import math

import jax
import jax.numpy as jnp
import numpy as np
from jax import lax
from jax.experimental import pallas as pl
from jax.experimental.pallas import tpu as pltpu
from jax.sharding import PartitionSpec as P

MESH = pl.DeviceIdType.MESH
F32 = jnp.float32
BF16 = jnp.bfloat16
NORM_EPSILON = 1e-05
FEATURES = 384
BLOCK = 48
FIELDS = 7
VMEM_BYTES = 63 * 1024 * 1024


def split_np(table):
    high = table.astype(np.float32).astype(jnp.bfloat16)
    low = (table - high.astype(np.float64)).astype(np.float32).astype(jnp.bfloat16)
    return high, low


def make_tables(ny, nz):
    chips = ny * nz
    n = 2 * chips
    scale = 1.0 / math.sqrt(n)
    pos = np.arange(n)
    angle = 2.0 * math.pi * ((pos[:, None] * pos[None, :]) % n) / n
    cosine, sine = np.cos(angle) * scale, np.sin(angle) * scale
    alternate = np.where(pos % 2 == 0, 1.0, -1.0) * scale
    lon_f = np.concatenate([cosine[:chips], -sine[:chips]], 0)
    lon_f[chips] = alternate
    y, z, a = np.meshgrid(np.arange(ny), np.arange(nz), np.arange(2), indexing="ij")
    row = (y * nz + z) * 2 + a
    arrive = row.transpose(1, 0, 2).reshape(-1)
    depart = row.transpose(0, 2, 1).reshape(-1)
    lat_f = np.concatenate([cosine[:, arrive], sine[:, arrive]], 1)
    lat_i = np.concatenate([cosine[depart], sine[depart]], 1)
    freq = (y * nz + z).transpose(1, 0, 2).reshape(-1)
    core = a.transpose(1, 0, 2).reshape(-1)
    imag = -sine[:, freq]
    imag[:, freq == 0] = alternate[:, None]
    lon_i = np.concatenate(
        [
            np.concatenate([np.where(core == b, cosine[:, freq], 0.0), np.where(core == b, imag, 0.0)], 1)
            for b in (0, 1)
        ],
        0,
    )
    group = 2 * ny
    perm = np.zeros((n, n))
    for s in range(group):
        for t in range(nz):
            perm[t * group + s, s * nz + t] = 1.0
    pack = np.zeros((12 * nz, 16 * nz))
    for t in range(nz):
        for u in range(6):
            pack[t * 6 + u, t * 16 + u] = 1.0
            pack[6 * nz + t * 6 + u, t * 16 + 8 + u] = 1.0
    narrow = np.concatenate([*split_np(lon_f), perm.astype(jnp.bfloat16)], 0)
    wide = np.concatenate([*split_np(lat_f), *split_np(lat_i), *split_np(lon_i)], 0)
    return narrow, wide, pack.astype(jnp.bfloat16)


def split(values):
    high = values.astype(BF16)
    return high, (values - high.astype(F32)).astype(BF16)


def dot(left, right):
    return jnp.dot(left, right, preferred_element_type=F32)


def dot_t(left, right):
    return lax.dot_general(left, right, (((1,), (1,)), ((), ())), preferred_element_type=F32)


def dot_3(left, right, op=dot):
    return op(left[0], right[0]) + (op(left[1], right[0]) + op(left[0], right[1]))


def normalise(values):
    centred = values - jnp.mean(values, axis=-1, keepdims=True)
    inverse = lax.rsqrt(jnp.mean(centred * centred, axis=-1, keepdims=True) + NORM_EPSILON)
    return centred * inverse, inverse


def norm_linear(normed, inverse, values):
    along = jnp.mean(normed * values, axis=-1, keepdims=True)
    return inverse * (values - jnp.mean(values, axis=-1, keepdims=True) - normed * along)


def gelu_parts(values):
    cumulative = 0.5 * (1.0 + lax.erf(values * (1.0 / math.sqrt(2.0))))
    density = jnp.exp(-0.5 * values * values) * (1.0 / math.sqrt(2.0 * math.pi))
    return values * cumulative, cumulative + values * density


def swap_parts(values):
    return jnp.concatenate(
        [values[:, 128:256], values[:, 0:128], pltpu.roll(values[:, 256:384], 64, 1)], axis=1
    )


def kernel(
    ny,
    nz,
    nx,
    *refs,
):
    inputs, (grad_ref, step_ref, ratio_ref), held, rest = refs[:15], refs[15:18], refs[18:33], refs[33:]
    (
        bg_ref,
        narrow_ref,
        dir_ref,
        mlp_in_ref,
        mlp_out_ref,
        wide_ref,
        spec_in_ref,
        spec_out_ref,
        pack_ref,
        owner_ref,
        cell_ref,
        count_ref,
        weight_ref,
        readout_ref,
        res_ref,
    ) = held
    (
        s1,
        r1,
        s2,
        r2,
        wz,
        win,
        wout,
        slope_ref,
        hidden,
        mixes,
        around,
        along,
        parts,
        sems,
        zsems,
        wsems,
        rsems,
        insems,
    ) = rest
    n = 2 * ny * nz
    chips = ny * nz
    group = 2 * ny
    lat = lax.axis_index("lat")
    ens = lax.axis_index("ens")
    core = lax.rem(lat, 2)
    chip = lax.div(lat, 2)
    yy = lax.div(chip, nz)
    zz = lax.rem(chip, nz)
    me_yc = yy * 2 + core

    def at_yc(k):
        return {"lat": (lax.div(k, 2) * nz + zz) * 2 + lax.rem(k, 2), "ens": ens}

    def at_z(t):
        return {"lat": (yy * nz + t) * 2 + core, "ens": ens}

    def at_x(t):
        return {"lat": lat, "ens": t}

    z_steps = sorted(range(1, nz), key=lambda s: (-min(s, nz - s), s))
    yc_partners = [
        lax.rem(yy + d, ny) * 2 + lax.rem(core + c, 2)
        for d, c in sorted(
            ((d, c) for d in range(ny) for c in (0, 1) if d or c), key=lambda p: -min(p[0], ny - p[0])
        )
    ]
    z_partners = [lax.rem(zz + s, nz) for s in z_steps]
    plane = [
        (lax.rem(me_yc + k, group), lax.rem(ens + t, nx))
        for k, t in sorted(
            ((k, t) for k in range(group) for t in range(nx) if k or t),
            key=lambda p: -min(p[0] // 2, ny - p[0] // 2) - min(p[1], nx - p[1]),
        )
    ]

    def at_plane(p):
        return {"lat": (lax.div(p[0], 2) * nz + zz) * 2 + lax.rem(p[0], 2), "ens": p[1]}

    for i in range(15):
        pltpu.make_async_copy(inputs[i], held[i], insems.at[i]).start()
    barrier = pltpu.get_barrier_semaphore()
    for t in z_partners:
        pl.semaphore_signal(barrier, inc=1, device_id=at_z(t), device_id_type=MESH)
    for p in plane:
        pl.semaphore_signal(barrier, inc=1, device_id=at_plane(p), device_id_type=MESH)

    ready = set()

    def load(*wanted):
        for ref in wanted:
            i = next(k for k in range(15) if held[k] is ref)
            if i not in ready:
                ready.add(i)
                pltpu.make_async_copy(inputs[i], ref, insems.at[i]).wait()

    leaving, coming = [], {}

    def push(source, target, send, recv, where):
        pltpu.make_async_remote_copy(
            src_ref=source,
            dst_ref=target,
            send_sem=send,
            recv_sem=recv,
            device_id=where,
            device_id_type=MESH,
        ).start()

    def wait_bytes(ref, sem):
        pltpu.make_async_copy(ref, ref, sem).wait()

    def arrive(key):
        wait_bytes(*coming.pop(key))

    def finish():
        load(*held)
        for key in list(coming):
            arrive(key)
        for ref, sem in leaving:
            wait_bytes(ref, sem)

    def phase_one(f):
        for k in yc_partners:
            push(s1.at[f, k], r1.at[f, me_yc], sems.at[f, 0], sems.at[f, 1], at_yc(k))
        pltpu.make_async_copy(s1.at[f, me_yc], r1.at[f, me_yc], sems.at[f, 1]).start()
        leaving.append((s1.at[f, pl.ds(0, group - 1)], sems.at[f, 0]))
        coming["one", f] = (r1.at[f], sems.at[f, 1])

    def phase_two(f):
        arrive(("one", f))
        turned = dot(narrow_ref[2 * n : 3 * n, :], r1[f].reshape(n, FEATURES))
        s2[f] = turned.reshape(nz, group, FEATURES).astype(BF16)
        for t in z_partners:
            push(s2.at[f, t], r2.at[f, zz], sems.at[f, 2], sems.at[f, 3], at_z(t))
        pltpu.make_async_copy(s2.at[f, zz], r2.at[f, zz], sems.at[f, 3]).start()
        leaving.append((s2.at[f, pl.ds(0, nz - 1)], sems.at[f, 2]))
        coming["two", f] = (r2.at[f], sems.at[f, 3])

    def received(f):
        arrive(("two", f))
        return r2[f].astype(F32).reshape(n, FEATURES)

    def lon_f():
        load(narrow_ref)
        return narrow_ref[0:n, :], narrow_ref[n : 2 * n, :]

    def lat_f():
        load(wide_ref)
        return wide_ref[0:n, :], wide_ref[n : 2 * n, :]

    def lat_i():
        return wide_ref[2 * n : 3 * n, :], wide_ref[3 * n : 4 * n, :]

    def lon_i():
        return wide_ref[4 * n : 6 * n, :], wide_ref[6 * n : 8 * n, :]

    lane = lax.broadcasted_iota(jnp.int32, (1, FEATURES), 1)
    low_half = lax.rem(lane, 128) < 64
    tail_real = low_half == (core == 0)
    mask_r = jnp.where(jnp.logical_or(lane < 128, jnp.logical_and(lane >= 256, tail_real)), 1.0, 0.0)
    mask_i = 1.0 - mask_r
    plain = jnp.where(chip == 0, 0.0, 1.0)
    first = 1.0 - plain
    low_lane = lax.broadcasted_iota(jnp.int32, (1, 128), 1) < 64

    def lon_forward(f, field):
        spectrum = dot_3(lon_f(), split(field))
        real, imag = spectrum[0:chips], spectrum[chips:n]
        imag_mid = pltpu.roll(imag[:, 128:256], 64, 1)
        real_mid = real[:, 128:256]
        for b in (0, 1):
            if b == 0:
                tiles = [real[:, 0:128], imag[:, 0:128], jnp.where(low_lane, real_mid, imag_mid)]
            else:
                tiles = [real[:, 256:384], imag[:, 256:384], jnp.where(low_lane, imag_mid, real_mid)]
            for i, tile in enumerate(tiles):
                low = tile.astype(BF16)
                for y in range(ny):
                    s1[f, 2 * y + b, :, i * 128 : (i + 1) * 128] = low[y * nz : (y + 1) * nz]

    def lon_inverse(f):
        values = received(f)
        tail = values[:, 256:384]
        stacked = jnp.concatenate(
            [
                jnp.concatenate([values[:, 0:128], tail], axis=1),
                jnp.concatenate([values[:, 128:256], pltpu.roll(tail, 64, 1)], axis=1),
            ],
            axis=0,
        ).astype(BF16)
        high, low = lon_i()
        out = dot(high, stacked) + dot(low, stacked)
        middle_tile = jnp.where(low_lane, out[0:n, 128:256], out[n : 2 * n, 128:256])
        return jnp.concatenate([out[0:n, 0:128], middle_tile, out[n : 2 * n, 0:128]], axis=1)

    def lat_forward(f):
        high, low = lat_f()
        x = received(f)
        sw = swap_parts(x)
        left = jnp.concatenate(
            [x * (mask_r + plain * mask_i), sw * (plain * mask_r - mask_i)], axis=0
        ).astype(BF16)
        right = jnp.concatenate(
            [
                x * (plain * mask_r - plain * mask_i) + sw * (first * mask_r),
                sw * (-plain) - x * (first * mask_i),
            ],
            axis=0,
        ).astype(BF16)
        return jnp.concatenate(
            [dot(high, left) + dot(low, left), dot(high, right) + dot(low, right)],
            axis=0,
        )

    def lat_inverse(f, both):
        a, b = both[0:n], both[n : 2 * n]
        sa, sb = swap_parts(a), swap_parts(b)
        upper = a * (mask_r + plain * mask_i) + b * (plain * (mask_r - mask_i)) + sb * (first * mask_i)
        lower = sa * (plain * mask_i - mask_r) - sb * plain - b * (first * mask_i)
        both_low = jnp.concatenate([upper, lower], axis=0).astype(BF16)
        high, low = lat_i()
        out = dot(high, both_low) + dot(low, both_low)
        s1[f] = out.reshape(group, nz, FEATURES).astype(BF16)

    def mix(values, which, op=dot):
        return op(values.astype(BF16), mixes[which])

    load(bg_ref)
    state = bg_ref[...].astype(F32)
    normed, inverse = normalise(state)
    lon_forward(0, normed)
    pick = lax.broadcasted_iota(jnp.int32, (16, 6), 0) - lax.broadcasted_iota(jnp.int32, (16, 6), 1)
    load(mlp_in_ref, mlp_out_ref)
    rows_in = dot(jnp.where(pick == 0, 1.0, 0.0).astype(BF16), mlp_in_ref[...])
    rows_out = dot(jnp.where(pick == 8, 1.0, 0.0).astype(BF16), mlp_out_ref[...])
    wz[lax.rem(zz, min(4, nz)), lax.div(zz, min(4, nz))] = (rows_in + rows_out).astype(BF16)
    load(dir_ref)
    heading = dir_ref[...]
    lon_forward(1, norm_linear(normed, inverse, heading))
    load(owner_ref, cell_ref, count_ref, weight_ref)
    rows = owner_ref.shape[1]
    owner_row = jnp.broadcast_to(owner_ref[...].astype(F32), (rows, rows))
    owner_col = owner_row.T
    cell_col = jnp.broadcast_to(cell_ref[...].astype(F32), (rows, rows)).T
    sub = lax.broadcasted_iota(jnp.int32, (rows, rows), 0)
    col = lax.broadcasted_iota(jnp.int32, (rows, rows), 1)
    again = jnp.where(jnp.logical_and(owner_col == owner_row, sub < col), 1.0, 0.0)
    rank = jnp.sum(again, axis=0, keepdims=True)
    slot = lax.broadcasted_iota(jnp.int32, (n, rows), 0)
    slot_k, slot_z = lax.div(slot, nz), lax.rem(slot, nz)
    slot_lat = (lax.div(slot_k, 2) * nz + slot_z) * 2 + lax.rem(slot_k, 2)
    mine = owner_row[0:1, :] == slot_lat.astype(F32)
    hit_a = jnp.where(jnp.logical_and(mine, rank == 0.0), 1.0, 0.0).astype(BF16)
    hit_b = jnp.where(jnp.logical_and(mine, rank == 1.0), 1.0, 0.0).astype(BF16)
    row_id = lax.broadcasted_iota(jnp.int32, weight_ref.shape, 0)
    weights = jnp.where(row_id < count_ref[...], weight_ref[...], 0.0).astype(BF16)
    cells = jnp.broadcast_to(cell_col[:, 0:1], (rows, 128)).astype(BF16)
    ids = jnp.where(low_lane, dot(hit_a, cells), dot(hit_b, cells))
    slots = jnp.concatenate([dot(hit_a, weights), dot(hit_b, weights), ids], axis=1)
    s1[2] = slots.reshape(group, nz, FEATURES).astype(BF16)
    pl.semaphore_wait(barrier, (nz - 1) + (group * nx - 1))
    phase_one(0)
    classes = min(4, nz)
    quads = nz // classes
    own_class, own_quad = lax.rem(zz, classes), lax.div(zz, classes)
    far = sorted(range(1, quads), key=lambda q: -min(q, quads - q))
    for q in far:
        target = lax.rem(zz + classes * q, nz)
        push(wz.at[own_class, own_quad], wz.at[own_class, own_quad], zsems.at[0], zsems.at[1], at_z(target))
    if far:
        leaving.append((wz.at[0, pl.ds(0, quads - 1)], zsems.at[0]))
        coming["quads"] = (wz.at[0, pl.ds(0, quads - 1)], zsems.at[1])
    phase_one(1)
    phase_one(2)
    phase_two(0)
    half = 4 * BLOCK
    p_row = lax.broadcasted_iota(jnp.int32, (FEATURES, 1), 0)

    def local_feature(p):
        within = lax.rem(p, 128)
        tail = lax.rem(p, 64)
        low_core = jnp.where(p < 256, within, 128 + tail)
        high_core = jnp.where(p < 256, 64 + within, tail)
        return jnp.where(core == 0, low_core, high_core)

    def block_of(u):
        return lax.div(u, BLOCK)

    row_tail_real = (lax.rem(p_row, 128) < 64) == (core == 0)
    row_real = jnp.logical_or(p_row < 128, jnp.logical_and(p_row >= 256, row_tail_real))
    u_row, u_lane = local_feature(p_row), local_feature(lane)
    spread = jnp.where(
        u_row == lax.broadcasted_iota(jnp.int32, (FEATURES, half), 1), 1.0, 0.0
    ).astype(BF16)
    widen = jnp.where(
        lax.broadcasted_iota(jnp.int32, (BLOCK, FEATURES), 0) == u_lane - BLOCK * block_of(u_lane), 1.0, 0.0
    ).astype(BF16)
    same_block = block_of(u_row) == block_of(u_lane)
    same_part = row_real == (mask_r > 0.5)
    cross_sign = jnp.where(row_real, 1.0, -1.0)
    load(spec_in_ref, spec_out_ref)
    for which, ref in ((0, spec_in_ref), (1, spec_out_ref)):
        real_low = ref[0, pl.ds(core * half, half), :].astype(BF16)
        imag_low = ref[1, pl.ds(core * half, half), :].astype(BF16)
        real_part = dot(dot(spread, real_low).astype(BF16), widen)
        imag_part = dot(dot(spread, imag_low).astype(BF16), widen)
        dense = jnp.where(same_part, real_part, imag_part * cross_sign)
        mixes[which] = jnp.where(same_block, dense, 0.0).astype(BF16)

    if far:
        arrive("quads")
    near = [1, nz - 1, 2][: classes - 1]
    for step in near:
        push(wz.at[own_class], wz.at[own_class], zsems.at[2], zsems.at[3], at_z(lax.rem(zz + step, nz)))
    if near:
        leaving.append((wz.at[pl.ds(0, classes - 1)], zsems.at[2]))
        coming["classes"] = (wz.at[pl.ds(0, classes - 1)], zsems.at[3])
    phase_two(1)
    six = 6 * nz
    sibling = at_yc(yy * 2 + (1 - core))

    class Gather:
        def __init__(self, ref, which, first, second, first_at, second_at, first_n, second_n):
            self.ref, self.sem, self.f, self.g = ref, lambda i: wsems.at[which, i], first, second
            self.which, self.first_at, self.second_at = which, first_at, second_at
            self.nf, self.ng = first_n, second_n
            self.left = lax.rem(second + second_n - 1, second_n)
            self.right = lax.rem(second + 1, second_n)
            self.order = sorted(range(first_n), key=lambda i: (min(i, first_n - i), i))

        def block(self, g, f):
            return self.ref.at[core, g, f] if self.which == 0 else self.ref.at[core, f, g]

        def slab(self, g):
            return self.ref.at[core, g] if self.which == 0 else self.ref.at[core, :, g]

        def blocks(self, count):
            part = pl.ds(0, count)
            return self.ref.at[0, 0, part] if self.which == 0 else self.ref.at[0, part, 0]

        def offset(self, i):
            return lax.rem(self.f + i, self.nf)

        def beside(self, i):
            mine = self.block(self.g, self.offset(i))
            if self.ng > 1:
                push(mine, mine, self.sem(4), self.sem(8 + i), self.second_at(self.right))
                coming["left", self, i] = (self.blocks(1), self.sem(8 + i))
            if self.ng > 2:
                push(mine, mine, self.sem(5), self.sem(12 + i), self.second_at(self.left))
                coming["right", self, i] = (self.blocks(1), self.sem(12 + i))

        def begin(self):
            mine = self.block(self.g, self.f)
            direct = [i for i in self.order[1:] if min(i, self.nf - i) == 1]
            for i in direct:
                push(mine, mine, self.sem(0), self.sem(self.nf - i), self.first_at(self.offset(i)))
            for i in self.order[1:]:
                coming["first", self, i] = (self.blocks(1), self.sem(i))
            self.beside(0)
            if self.nf > 1:
                leaving.append((self.blocks(len(direct)), self.sem(0)))
            if self.nf > 2:
                leaving.append((self.blocks(1), self.sem(24)))
            if self.ng > 1:
                leaving.append((self.blocks(self.nf), self.sem(4)))
            if self.ng > 2:
                leaving.append((self.blocks(self.nf), self.sem(5)))

        def spread(self, i):
            arrive(("first", self, i))
            if self.nf > 2 and i != 2:
                half = six // 2
                ref = self.block(self.g, self.offset(i)).at[pl.ds(0 if i == 1 else half, half)]
                push(ref, ref, self.sem(24), self.sem(2), self.first_at(self.offset(self.nf - i)))
            self.beside(i)

        def cross(self, g, i):
            slab = self.slab(g)
            push(slab, slab, self.sem(16 + 2 * i), self.sem(17 + 2 * i), sibling)
            leaving.append((slab, self.sem(16 + 2 * i)))
            coming["core", self, i] = (slab, self.sem(17 + 2 * i))

        def pass_on(self, i):
            half = six // 2
            for key, origin, target, part in (
                ("left", self.left, self.right, pl.ds(0, half)),
                ("right", self.right, self.left, pl.ds(half, half)),
            ):
                if (key, self, i) in coming:
                    arrive((key, self, i))
                if self.ng > 2:
                    ref = self.block(origin, self.offset(i)).at[part]
                    push(ref, ref, self.sem(6), self.sem(7), self.second_at(target))
            if i == self.order[-1]:
                if self.ng > 2:
                    leaving.append((self.blocks(self.nf), self.sem(6)))
                    coming["opposite", self] = (self.blocks(self.nf), self.sem(7))
                if self.ng > 1:
                    self.cross(self.left, 1)
                if self.ng > 2:
                    self.cross(self.right, 2)

        def last(self):
            if self.ng > 2:
                arrive(("opposite", self))
                self.cross(lax.rem(self.g + 2, self.ng), 3)

        def slabs(self):
            return [self.g, self.left, self.right, lax.rem(self.g + 2, self.ng)][: self.ng]

    def at_y(t):
        return at_yc(t * 2 + core)

    gather_in = Gather(win, 0, yy, ens, at_y, at_x, ny, nx)
    gather_out = Gather(wout, 1, ens, yy, at_x, at_y, nx, ny)
    before = mix(lat_forward(0), 0)
    value, spec_slope = gelu_parts(before)
    lat_inverse(3, mix(value, 1))
    phase_one(3)
    if near:
        arrive("classes")
    load(pack_ref)
    packed = dot(pack_ref[...], wz[...].reshape(16 * nz, FEATURES)).astype(BF16)
    win[core, ens, yy] = packed[0:six]
    wout[core, ens, yy] = packed[six : 2 * six]
    gather_in.begin()
    gather_out.begin()
    phase_two(2)
    phase_two(3)

    lat_inverse(4, mix(spec_slope * mix(lat_forward(1), 0), 1))
    phase_one(4)
    for i in range(1, max(nx, ny)):
        for gather in (gather_in, gather_out):
            if i < gather.nf:
                gather.spread(gather.order[i])
    phase_two(4)
    for gather in (gather_in, gather_out):
        gather.cross(gather.g, 0)
    got = received(2)
    cell_id = lax.broadcasted_iota(jnp.int32, (n, n), 1).astype(F32)
    at_a = jnp.where(got[:, 256:257] == cell_id, 1.0, 0.0)
    at_b = jnp.where(got[:, 320:321] == cell_id, 1.0, 0.0)
    cell_weights = dot(at_a.T.astype(BF16), got[:, 0:128].astype(BF16)) + dot(
        at_b.T.astype(BF16), got[:, 128:256].astype(BF16)
    )

    for i in range(max(nx, ny)):
        for gather in (gather_in, gather_out):
            if i < gather.nf:
                gather.pass_on(gather.order[i])

    middle = state + lon_inverse(3)
    mixed, mixed_inverse = normalise(middle)
    mixed_low = mixed.astype(BF16)

    units = ny * six

    def slope_of(co, g):
        block = win[co, g].reshape(units, FEATURES)
        slope_ref[co * nx + g] = gelu_parts(dot_t(mixed_low, block))[1]

    slabs = gather_in.slabs()
    slope_of(core, slabs[0])
    arrive(("core", gather_in, 0))
    slope_of(1 - core, slabs[0])
    for i in range(1, min(3, nx)):
        slope_of(core, slabs[i])
    tangent_middle = heading + lon_inverse(4)
    tangent_low = norm_linear(mixed, mixed_inverse, tangent_middle).astype(BF16)
    gather_in.last()
    gather_out.last()
    for i in range(1, nx):
        if i == 3:
            slope_of(core, slabs[i])
        arrive(("core", gather_in, i))
        slope_of(1 - core, slabs[i])
    for i in range(ny):
        arrive(("core", gather_out, i))

    def through(values_low, ref):
        for i in range(2 * nx):
            block = ref[i // nx, i % nx].reshape(units, FEATURES)
            hidden[:, i * units : (i + 1) * units] = (slope_ref[i] * dot_t(values_low, block)).astype(BF16)
        return hidden[...]

    tangent_out = tangent_middle + dot(through(tangent_low, win), wout[...].reshape(-1, FEATURES))
    load(readout_ref)
    readout = split(readout_ref[...])
    departures = dot_3(split(tangent_out), readout)
    gradient = dot_3(split(cell_weights * departures), readout, dot_t)
    gradient_low = gradient.astype(BF16)

    grad_mixed = dot(through(gradient_low, wout), win[...].reshape(-1, FEATURES))
    grad_middle = gradient + norm_linear(mixed, mixed_inverse, grad_mixed)

    lon_forward(5, grad_middle)
    phase_one(5)
    phase_two(5)
    lat_inverse(6, mix(spec_slope * mix(lat_forward(5), 1, dot_t), 0, dot_t))
    phase_one(6)
    phase_two(6)
    update = grad_middle + norm_linear(normed, inverse, lon_inverse(6))
    grad_ref[...] = update

    load(res_ref)
    residual = res_ref[...]
    hessian = heading + update
    sums = [
        jnp.sum(jnp.sum(v, axis=0, keepdims=True), axis=1, keepdims=True)
        for v in (residual * residual, heading * hessian, residual * hessian, hessian * hessian)
    ]
    place = lax.broadcasted_iota(jnp.int32, (1, 128), 1)
    total = jnp.zeros((1, 128), F32)
    for i, value in enumerate(sums):
        total = total + jnp.where(place == i, value, 0.0)

    def reduce_over(i, total, buffer, mine_at, partners, where):
        parts[i] = total
        for t in partners:
            push(parts.at[i], buffer.at[mine_at], rsems.at[i, 0], rsems.at[i, 1], where(t))
        pltpu.make_async_copy(parts.at[i], buffer.at[mine_at], rsems.at[i, 1]).start()
        leaving.append((buffer.at[pl.ds(0, len(partners))], rsems.at[i, 0]))
        wait_bytes(buffer, rsems.at[i, 1])
        return jnp.sum(buffer[...], axis=0)

    total = reduce_over(0, total, around, me_yc * nx + ens, plane, at_plane)
    total = reduce_over(1, total, along, zz, z_partners, at_z)
    norm_now, curvature, cross, square = total[:, 0:1], total[:, 1:2], total[:, 2:3], total[:, 3:4]
    step = norm_now / curvature
    norm_next = norm_now + step * (step * square - 2.0 * cross)
    ratio = norm_next / norm_now
    step_ref[...] = jnp.broadcast_to(step, step_ref.shape)
    ratio_ref[...] = jnp.broadcast_to(ratio, ratio_ref.shape)
    finish()


def per_device(ny, nz, nx, background, increment, residual, direction, spec_in, spec_out, mlp_in,
               mlp_out, readout, obs_owner, obs_cell, obs_count, obs_weight):
    n = background.shape[2]
    group = 2 * ny
    six = 6 * nz
    narrow, wide, pack = make_tables(ny, nz)
    vmem = pl.BlockSpec(memory_space=pltpu.VMEM)
    operands = (
        background.reshape(n, FEATURES),
        jnp.asarray(narrow),
        direction.reshape(n, FEATURES),
        mlp_in.T,
        mlp_out,
        jnp.asarray(wide),
        spec_in.reshape(2, FEATURES, BLOCK),
        spec_out.reshape(2, FEATURES, BLOCK),
        jnp.asarray(pack),
        obs_owner.reshape(1, -1),
        obs_cell.reshape(1, -1),
        obs_count.reshape(1, 1),
        obs_weight,
        readout,
        residual.reshape(n, FEATURES),
    )
    update, step, ratio = pl.pallas_call(
        functools.partial(kernel, ny, nz, nx),
        out_shape=(
            jax.ShapeDtypeStruct((n, FEATURES), F32),
            jax.ShapeDtypeStruct((n, FEATURES), F32),
            jax.ShapeDtypeStruct((n, FEATURES), F32),
        ),
        in_specs=[pl.BlockSpec(memory_space=pl.ANY)] * 15,
        out_specs=(vmem, vmem, vmem),
        scratch_shapes=[pltpu.VMEM(v.shape, v.dtype) for v in operands]
        + [
            pltpu.VMEM((FIELDS, group, nz, FEATURES), BF16),
            pltpu.VMEM((FIELDS, group, nz, FEATURES), BF16),
            pltpu.VMEM((FIELDS, nz, group, FEATURES), BF16),
            pltpu.VMEM((FIELDS, nz, group, FEATURES), BF16),
            pltpu.VMEM((min(4, nz), nz // min(4, nz), 16, FEATURES), BF16),
            pltpu.VMEM((2, nx, ny, six, FEATURES), BF16),
            pltpu.VMEM((2, nx, ny, six, FEATURES), BF16),
            pltpu.VMEM((2 * nx, n, ny * six), F32),
            pltpu.VMEM((n, 2 * nx * ny * six), BF16),
            pltpu.VMEM((2, FEATURES, FEATURES), BF16),
            pltpu.VMEM((group * nx, 1, 128), F32),
            pltpu.VMEM((nz, 1, 128), F32),
            pltpu.VMEM((2, 1, 128), F32),
            pltpu.SemaphoreType.DMA((FIELDS, 4)),
            pltpu.SemaphoreType.DMA((4,)),
            pltpu.SemaphoreType.DMA((2, 25)),
            pltpu.SemaphoreType.DMA((2, 2)),
            pltpu.SemaphoreType.DMA((15,)),
        ],
        compiler_params=pltpu.CompilerParams(
            collective_id=0, has_side_effects=True, vmem_limit_bytes=VMEM_BYTES
        ),
    )(*operands)
    step, ratio = (v.reshape(direction.shape) for v in (step, ratio))
    hessian_dir = direction + update.reshape(direction.shape)
    residual_new = residual - step * hessian_dir
    return (
        increment + step * direction,
        residual_new,
        residual_new + ratio * direction,
        hessian_dir,
    )


def solution(mesh):
    n_lat, nx = mesh.shape["lat"], mesh.shape["ens"]
    nz = 16 if n_lat == 128 else 2
    ny = n_lat // (2 * nz)
    field = P("ens", "lat", None, None)
    return jax.shard_map(
        functools.partial(per_device, ny, nz, nx),
        mesh=mesh,
        in_specs=(
            field,
            field,
            field,
            field,
            P(),
            P(),
            P(None, ("lat", "ens")),
            P(("lat", "ens"), None),
            P(),
            P("lat", None),
            P("lat"),
            P("lat"),
            P("lat", None),
        ),
        out_specs=(field, field, field, field),
        check_vma=False,
    )
```
